128 devices in a mesh: gx: 8 (over y, core), gy: 16 (over x, z).
Axes of the slice: x: 4, y: 4, z: 4, core: 2. Of those that a mesh axis runs over, the one named last changes fastest.
Arguments:
- field: bfloat16 [20, 128, 128, 1024], P(None, 'gx', 'gy'), may hold values from -6 to 6
- spectral_weight: bfloat16 [2, 128, 20, 20, 1024], P(None, ('gx', 'gy')), may hold values from -1 to 1
- bypass_weight: bfloat16 [20, 20], replicated, may hold values from -1.25 to 1.25
- bypass_bias: float32 [20], replicated, may hold values from -3 to 3
- cotangent: bfloat16 [20, 128, 128, 1024], P(None, 'gx', 'gy'), may hold values from -1.5 to 1.5
Outputs:
- out_field: bfloat16 [20, 128, 128, 1024], P(None, 'gx', 'gy')
- field_grad: bfloat16 [20, 128, 128, 1024], P(None, 'gx', 'gy')
- spectral_grad: bfloat16 [2, 128, 20, 20, 1024], P(None, ('gx', 'gy'))
- bypass_grad: float32 [20, 20], replicated
- bias_grad: float32 [20], replicated
The draws below stay inside these ranges and needn't reach their ends.
All inputs are finite; a program needn't handle non-finite values.
Results may differ from the reference program's by a relative error of at most 0.022.
Values may be sent and summed in bfloat16 or wider, within the bound.
No kernel may reach another device: no remote copies, remote signals or barrier semaphores. Data moves between devices by JAX's collectives and lax.ppermute only.
A program may use at most 192 MiB of HBM per device.

```python
import math
import jax
import jax.numpy as jnp
from jax import lax

C = 20
NX = 128
NY = 128
NZ = 64
NT = 16
MX = 32
MY = 32
MZ = 16
MT = 8
ZT = 1024
MZT = 128
KXY = 1024


def shard_levels(rng, extent, cuts, least, high):
    def one(axis_at, shards_of):
        steps = jax.random.uniform(jax.random.fold_in(jax.random.fold_in(rng, 6), axis_at), (shards_of,), jnp.float32, least / len(cuts), high / len(cuts))
        return jnp.repeat(jnp.exp(steps), extent[axis_at] // shards_of).reshape((-1,) + (1,) * (len(extent) - axis_at - 1))

    loudness = one(*cuts[0])
    for cut in cuts[1:]:
        loudness = loudness * one(*cut)
    return loudness


def bell_draw(stream_key, extent, scale, most, cuts=(), held_as=jnp.bfloat16):
    drawn = scale * jax.random.normal(stream_key, extent, jnp.float32)
    if cuts:
        drawn = drawn * shard_levels(stream_key, extent, cuts, -0.22, 0.18)
    return jnp.clip(drawn, -most, most).astype(held_as)


def setup_inputs(seed: int = 0) -> dict:
    key_of = jax.random.split(jax.random.key(seed), 6)
    field = bell_draw(key_of[0], (C, NX, NY, ZT), 1.0, 6.0, ((1, 8), (2, 16)))
    spectral_weight = bell_draw(key_of[1], (2, MZT, C, C, KXY), (2 * C) ** -0.5, 1.0, ((1, 128),))
    bypass_weight = bell_draw(key_of[2], (C, C), C ** -0.5, 1.25)
    bypass_bias = bell_draw(key_of[3], (C,), 0.5, 3.0, (), jnp.float32)
    cotangent = bell_draw(key_of[4], (C, NX, NY, ZT), 0.25, 1.5, ((1, 8), (2, 16)))
    return dict(field=field, spectral_weight=spectral_weight, bypass_weight=bypass_weight, bypass_bias=bypass_bias, cotangent=cotangent)


def mode_numbers(count):
    index = jnp.arange(count, dtype=jnp.int32)
    return jnp.where(index < count // 2, index, index - count)

def line_tables(length, kept):
    freqs = mode_numbers(kept)
    points = jnp.arange(length, dtype=jnp.int32)
    angle = 2.0 * math.pi / length * (freqs[:, None] * points[None, :] % length).astype(jnp.float32)
    cosine = jnp.cos(angle)
    sine = jnp.sin(angle)
    forward = jnp.stack([jnp.stack([cosine, sine], -1), jnp.stack([-sine, cosine], -1)], 1) / math.sqrt(length)
    cos_t = cosine.T
    sin_t = sine.T
    inverse = jnp.stack([jnp.stack([cos_t, -sin_t], -1), jnp.stack([sin_t, cos_t], -1)], 1) / math.sqrt(kept)
    return (forward.astype(jnp.bfloat16), inverse.astype(jnp.bfloat16))

def plane_tables():
    z_freq = mode_numbers(MZ)
    t_freq = jnp.arange(MT, dtype=jnp.int32)
    z_pos = jnp.arange(NZ, dtype=jnp.int32)
    t_pos = jnp.arange(NT, dtype=jnp.int32)
    turn_z = (z_pos[:, None] * z_freq[None, :] % NZ).astype(jnp.float32) / NZ
    turn_t = (t_pos[:, None] * t_freq[None, :] % NT).astype(jnp.float32) / NT
    angle = 2.0 * math.pi * (turn_z[:, None, :, None] + turn_t[None, :, None, :])
    parts = jnp.stack([jnp.cos(angle), -jnp.sin(angle)], -1)
    factor = jnp.where(t_freq == 0, 1.0, 2.0).astype(jnp.float32)
    forward = parts.reshape(NZ * NT, MZ * MT * 2) / math.sqrt(NZ * NT)
    inverse = (parts * factor[:, None]).reshape(NZ * NT, MZ * MT * 2).T / math.sqrt(2 * MZ * MT)
    return (forward.astype(jnp.bfloat16), inverse.astype(jnp.bfloat16))

def adjoint(table):
    return jnp.transpose(table, (2, 3, 0, 1))

def along(table, values, axis_pos):
    chans, first, second, pairs = values.shape
    split = values.reshape(chans, first, second, pairs // 2, 2).astype(jnp.float32)
    tab32 = table.astype(jnp.float32)
    if axis_pos == 1:
        result = jnp.einsum('paqb,cqymb->cpyma', tab32, split)
    else:
        result = jnp.einsum('paqb,cxqmb->cxpma', tab32, split)
    return result.reshape(result.shape[0], result.shape[1], result.shape[2], pairs).astype(jnp.bfloat16)

def to_modes(values, x_table, y_table):
    return along(y_table, along(x_table, values, 1), 2)

def to_grid(values, y_table, x_table):
    return along(x_table, along(y_table, values, 2), 1)

def split_modes(values):
    return values.reshape(values.shape[0], MX * MY, MZ * MT, 2).astype(jnp.float32)

def mix_forward(weight, spec_in):
    w_real = weight[0].astype(jnp.float32)
    w_imag = weight[1].astype(jnp.float32)
    parts = split_modes(spec_in)
    real_in = parts[..., 0]
    imag_in = parts[..., 1]
    real_out = jnp.einsum('mijk,ikm->jkm', w_real, real_in) - jnp.einsum('mijk,ikm->jkm', w_imag, imag_in)
    imag_out = jnp.einsum('mijk,ikm->jkm', w_real, imag_in) + jnp.einsum('mijk,ikm->jkm', w_imag, real_in)
    joined = jnp.stack([real_out, imag_out], -1)
    return joined.reshape(joined.shape[0], MX, MY, MZ * MT * 2).astype(jnp.bfloat16)

def mix_backward(weight, spec_in, back_modes):
    w_real = weight[0].astype(jnp.float32)
    w_imag = weight[1].astype(jnp.float32)
    parts = split_modes(spec_in)
    real_in = parts[..., 0]
    imag_in = parts[..., 1]
    grads = split_modes(back_modes)
    real_back = grads[..., 0]
    imag_back = grads[..., 1]
    real_grad = jnp.einsum('mijk,jkm->ikm', w_real, real_back) + jnp.einsum('mijk,jkm->ikm', w_imag, imag_back)
    imag_grad = jnp.einsum('mijk,jkm->ikm', w_real, imag_back) - jnp.einsum('mijk,jkm->ikm', w_imag, real_back)
    joined = jnp.stack([real_grad, imag_grad], -1)
    mode_grad = joined.reshape(joined.shape[0], MX, MY, MZ * MT * 2).astype(jnp.bfloat16)
    grad_real = jnp.einsum('ikm,jkm->mijk', real_in, real_back) + jnp.einsum('ikm,jkm->mijk', imag_in, imag_back)
    grad_imag = jnp.einsum('ikm,jkm->mijk', real_in, imag_back) - jnp.einsum('ikm,jkm->mijk', imag_in, real_back)
    return (mode_grad, jnp.stack([grad_real, grad_imag], 0).astype(jnp.bfloat16))

def join_blocks(stacked):
    moved = jnp.moveaxis(stacked, 0, 1)
    return moved.reshape((stacked.shape[1], NX) + stacked.shape[3:])

def reference(field, spectral_weight, bypass_weight, bypass_bias, cotangent):
    fwd_zt, inv_zt = plane_tables()
    fwd_x, inv_x = line_tables(NX, MX)
    fwd_y, inv_y = line_tables(NY, MY)
    plane_coef = jnp.dot(field, fwd_zt, preferred_element_type=jnp.float32).astype(jnp.bfloat16)
    spec_in = to_modes(plane_coef, fwd_x, fwd_y)
    spec_out = mix_forward(spectral_weight, spec_in)
    grid_coef = to_grid(spec_out, inv_y, inv_x)
    block = math.gcd(NX, 16)
    count = NX // block
    weight32 = bypass_weight.astype(jnp.float32)

    def tail(index):
        start = (index * block).astype(jnp.int32)
        field_blk = lax.dynamic_slice_in_dim(field, start, block, 1)
        coef_blk = lax.dynamic_slice_in_dim(grid_coef, start, block, 1)
        cot_blk = lax.dynamic_slice_in_dim(cotangent, start, block, 1)
        spectral = jnp.dot(coef_blk, inv_zt, preferred_element_type=jnp.float32)
        bypass = jnp.einsum('io,ixyz->oxyz', weight32, field_blk.astype(jnp.float32))
        pre = spectral + bypass + bypass_bias[:, None, None, None]
        output = jax.nn.gelu(pre).astype(jnp.bfloat16)
        unused, pull = jax.vjp(jax.nn.gelu, pre)
        grad_pre = pull(cot_blk.astype(jnp.float32))[0].astype(jnp.bfloat16)
        back_coef = jnp.dot(grad_pre, inv_zt.T, preferred_element_type=jnp.float32).astype(jnp.bfloat16)
        weight_part = jnp.einsum('ixyz,oxyz->io', field_blk.astype(jnp.float32), grad_pre.astype(jnp.float32))
        bias_part = lax.optimization_barrier(jnp.sum(grad_pre.astype(jnp.float32), axis=(1, 2, 3)))
        return (output, grad_pre, back_coef, weight_part, bias_part)
    outputs = lax.map(tail, jnp.arange(count, dtype=jnp.int32))
    out_field = join_blocks(outputs[0])
    grad_pre = join_blocks(outputs[1])
    back_coef = join_blocks(outputs[2])
    scale = 1.0 / math.sqrt(NX * NY * ZT)
    bypass_grad = lax.optimization_barrier(jnp.sum(outputs[3], 0)) * scale
    bias_grad = lax.optimization_barrier(jnp.sum(outputs[4], 0)) * scale
    back_modes = to_modes(back_coef, adjoint(inv_x), adjoint(inv_y))
    mode_grad, spectral_grad = mix_backward(spectral_weight, spec_in, back_modes)
    cell_grad = to_grid(mode_grad, adjoint(fwd_y), adjoint(fwd_x))

    def finish(index):
        start = (index * block).astype(jnp.int32)
        cell_blk = lax.dynamic_slice_in_dim(cell_grad, start, block, 1)
        pre_blk = lax.dynamic_slice_in_dim(grad_pre, start, block, 1)
        total = jnp.dot(cell_blk, fwd_zt.T, preferred_element_type=jnp.float32)
        total = total + jnp.einsum('io,oxyz->ixyz', weight32, pre_blk.astype(jnp.float32))
        return total.astype(jnp.bfloat16)
    field_grad = join_blocks(lax.map(finish, jnp.arange(count, dtype=jnp.int32)))
    return (out_field, field_grad, spectral_grad, bypass_grad, bias_grad)
```

```python
import math

import jax
import jax.numpy as jnp
import ml_dtypes
import numpy as np
from jax import lax
from jax.experimental import pallas as pl
from jax.experimental.pallas import tpu as pltpu
from jax.sharding import PartitionSpec as P

NX = 128
NY = 128
NZ = 64
NT = 16
MX = 32
MY = 32
MZ = 16
MT = 8
CH = 20
GX = 8
GY = 16
LX = NX // GX
LY = NY // GY
XY = LX * LY
ZT = NZ * NT
PAIRS = 2 * MZ * MT
MODES = MZ * MT
HI = CH // 4
AXES = ("gx", "gy")
BF = jnp.bfloat16
F32 = jnp.float32
MIB = 1 << 20


def mode_numbers(count):
    index = np.arange(count)
    return np.where(index < count // 2, index, index - count)


def plane_tables():
    z_freq = mode_numbers(MZ)
    t_freq = np.arange(MT)
    turn_z = (np.arange(NZ)[:, None] * z_freq[None, :] % NZ).astype(np.float32) / np.float32(NZ)
    turn_t = (np.arange(NT)[:, None] * t_freq[None, :] % NT).astype(np.float32) / np.float32(NT)
    angle = np.float32(2.0 * math.pi) * (turn_z[:, None, :, None] + turn_t[None, :, None, :])
    parts = np.stack([np.cos(angle), -np.sin(angle)], -1)
    factor = np.where(t_freq == 0, 1.0, 2.0).astype(np.float32)
    forward = parts.reshape(ZT, PAIRS) / np.float32(math.sqrt(ZT))
    inverse = (parts * factor[:, None]).reshape(ZT, PAIRS).T / np.float32(math.sqrt(PAIRS))
    return (forward.astype(ml_dtypes.bfloat16), inverse.astype(ml_dtypes.bfloat16))


def line_parts(length, kept):
    freqs = mode_numbers(kept)
    turns = (freqs[:, None] * np.arange(length)[None, :] % length).astype(np.float32)
    angle = np.float32(2.0 * math.pi / length) * turns
    norm = np.float32(math.sqrt(length))
    return (np.cos(angle) / norm, np.sin(angle) / norm)


def x_table():
    parts = np.stack(line_parts(NX, MX)).reshape(2, MX // 4, 4, GX, LX)
    table = np.einsum("phajw,vz->pvahjwz", parts, np.eye(LY, dtype=np.float32))
    return table.reshape(2 * LY * MX, GX * XY)


def y_table():
    cosine, sine = line_parts(NY, MY)
    block = np.stack(
        [
            np.stack([np.stack([cosine, -sine]), np.stack([sine, cosine])]),
            np.stack([np.stack([-sine, -cosine]), np.stack([cosine, -sine])]),
        ]
    )
    block = block.reshape(2, 2, 2, MY, GY, LY)
    table = np.einsum("sqpbkv,cd->svkcqdpb", block, np.eye(4, dtype=np.float32))
    return table.reshape(2 * LY * GY * 8, 8 * MY)


def spread_table():
    table = np.zeros((4, 4, MY, 4, 4, MY), np.float32)
    for low in range(4):
        for c in range(4):
            table[low, c, :, c, low, :] = np.eye(MY)
    return table.reshape(16 * MY, 16 * MY)


def pack_table(rows):
    table = np.zeros((8, rows, CH, 8, 2), np.float32)
    for m in range(8):
        for ch in range(CH):
            for r in range(2):
                table[m, 2 * ch + r, ch, m, r] = 1
    return table.reshape(8 * rows, CH * 16)


def fold_table():
    table = np.zeros((6, 8, 48), np.float32)
    for slot in range(42):
        table[slot % 6, slot // 6, slot if slot < 21 else slot + 3] = 1
    return table


def const(table):
    return jnp.asarray(np.asarray(table, np.float32).astype(ml_dtypes.bfloat16))


def dot(left, right, dims=((1,), (0,))):
    return lax.dot_general(left, right, (dims, ((), ())), preferred_element_type=F32)


def call(kernel, out, grid=None, limit=32, **kw):
    return pl.pallas_call(
        kernel,
        out_shape=out,
        grid=grid or (),
        compiler_params=pltpu.CompilerParams(vmem_limit_bytes=limit * MIB),
        **kw,
    )


def whole(shape):
    return pl.BlockSpec(shape, lambda *_: (0,) * len(shape))


def pack(coef, perm, out_ref):
    for b in range(0, MODES // 8, 2):
        sides = [coef[:, 16 * (b + e) : 16 * (b + e) + 16].reshape(16 * CH, XY) for e in range(2)]
        moved = dot(perm, jnp.concatenate(sides, 1)).astype(BF)
        for e in range(2):
            out_ref[(b + e) * 320 : (b + e + 1) * 320] = moved[:, e * XY : (e + 1) * XY]


def unpack(msg_ref, perm, rows, flat, coef):
    for b in range(0, MODES // 8, 2):
        sides = [msg_ref[(b + e) * 8 * rows : (b + e + 1) * 8 * rows] for e in range(2)]
        moved = dot(perm, jnp.concatenate(sides, 1)).astype(BF)
        for e in range(2):
            part = moved[:, e * XY : (e + 1) * XY].reshape(CH, 16, XY)
            flat[:, 16 * (b + e) : 16 * (b + e) + 16] = part
    for ch in range(CH):
        coef[ch] = flat[ch].T.reshape(LX, LY, PAIRS)


def first_kernel(field_ref, table_ref, perm_ref, out_ref, flat):
    g = pl.program_id(0)
    block = field_ref.shape[0]
    coef = dot(field_ref[...].reshape(block * XY, ZT), table_ref[...]).astype(BF)
    for c in range(block):
        flat[pl.ds(g * block + c, 1)] = coef[c * XY : (c + 1) * XY].T[None]

    @pl.when(g == pl.num_programs(0) - 1)
    def _():
        pack(flat, perm_ref[...], out_ref)


def plane_stage(field, table, perm):
    block = 4
    return call(
        first_kernel,
        jax.ShapeDtypeStruct((MODES * 2 * CH, XY), BF),
        grid=(CH // block,),
        limit=56,
        in_specs=[
            pl.BlockSpec((block, XY, ZT), lambda g: (g, 0, 0)),
            whole(table.shape),
            whole(perm.shape),
        ],
        out_specs=whole((MODES * 2 * CH, XY)),
        scratch_shapes=[pltpu.VMEM((CH, PAIRS, XY), BF)],
    )(field, table, perm)


def modes_in(msg_ref, x_ref, y_ref, spread_ref, scale):
    rows = [
        jnp.concatenate([msg_ref[j, :, hi].reshape(GY * 8, XY) for j in range(GX)], 1)
        for hi in range(HI)
    ]
    after_x = dot(x_ref[...], jnp.concatenate(rows, 0), ((1,), (1,))).astype(BF)
    left = jnp.concatenate(
        [
            jnp.concatenate(
                [after_x[s * MX : (s + 1) * MX, hi * 128 : (hi + 1) * 128] for s in range(2 * LY)], 1
            )
            for hi in range(HI)
        ],
        0,
    )
    after_y = dot(left, y_ref[...]) * scale
    grouped = jnp.concatenate(
        [
            jnp.concatenate(
                [
                    after_y[hi * MX + 8 * low : hi * MX + 8 * low + 8, t * 128 : (t + 1) * 128]
                    for low in range(4)
                ],
                1,
            )
            for t in range(2)
            for hi in range(HI)
        ],
        0,
    ).astype(BF)
    spread = dot(grouped, spread_ref[...])
    found = {}
    for t in range(2):
        for hi in range(HI):
            for c in range(4):
                at = 4 * t + c
                row = (t * HI + hi) * 8
                found[hi * 4 + at // 2, at % 2] = spread[row : row + 8, c * 128 : (c + 1) * 128]
    return found


def modes_out(found, x_ref, y_back_ref, gather_ref, out_ref):
    rows = []
    for t in range(2):
        for hi in range(HI):
            tiles = []
            for c in range(4):
                at = 4 * t + c
                tiles.append(found[hi * 4 + at // 2, at % 2])
            rows.append(jnp.concatenate(tiles, 1))
    gathered = dot(jnp.concatenate(rows, 0).astype(BF), gather_ref[...])
    grouped = jnp.concatenate(
        [
            jnp.concatenate(
                [
                    gathered[(t * HI + hi) * 8 : (t * HI + hi) * 8 + 8, low * 128 : (low + 1) * 128]
                    for t in range(2)
                ],
                1,
            )
            for hi in range(HI)
            for low in range(4)
        ],
        0,
    ).astype(BF)
    after_y = dot(grouped, y_back_ref[...]).astype(BF)
    left = jnp.concatenate(
        [
            jnp.concatenate(
                [
                    after_y[hi * MX : (hi + 1) * MX, s * 128 : (s + 1) * 128]
                    for hi in range(HI)
                ],
                1,
            )
            for s in range(2 * LY)
        ],
        0,
    )
    after_x = dot(left.T, x_ref[...]).astype(BF)
    for j in range(GX):
        for hi in range(HI):
            block = after_x[hi * 128 : (hi + 1) * 128, j * XY : (j + 1) * XY]
            out_ref[j, :, hi] = block.reshape(GY, 8, XY)


def mix_kernel(msg_ref, w_ref, x_ref, y_ref, y_back_ref, spread_ref, gather_ref, out_ref, spec_ref):
    spec = modes_in(msg_ref, x_ref, y_ref, spread_ref, 1.0)
    for i in range(CH):
        for r in range(2):
            spec_ref[i, r] = spec[i, r]
    mixed = {}
    for o in range(CH):
        real = jnp.zeros((8, 128), F32)
        imag = jnp.zeros((8, 128), F32)
        for i in range(CH):
            w_real = w_ref[0, i, o].astype(F32)
            w_imag = w_ref[1, i, o].astype(F32)
            real += w_real * spec[i, 0] - w_imag * spec[i, 1]
            imag += w_real * spec[i, 1] + w_imag * spec[i, 0]
        mixed[o, 0] = 4.0 * real
        mixed[o, 1] = 4.0 * imag
    modes_out(mixed, x_ref, y_back_ref, gather_ref, out_ref)


def mix_back_kernel(
    msg_ref, w_ref, spec_ref, sums_ref, x_ref, y_ref, y_back_ref, spread_ref, gather_ref, out_ref, grad_ref
):
    back = modes_in(msg_ref, x_ref, y_ref, spread_ref, 4.0)
    mixed = {}
    for i in range(CH):
        real = jnp.zeros((8, 128), F32)
        imag = jnp.zeros((8, 128), F32)
        in_real = spec_ref[i, 0]
        in_imag = spec_ref[i, 1]
        for o in range(CH):
            w_real = w_ref[0, i, o].astype(F32)
            w_imag = w_ref[1, i, o].astype(F32)
            real += w_real * back[o, 0] + w_imag * back[o, 1]
            imag += w_real * back[o, 1] - w_imag * back[o, 0]
            grad_ref[0, i, o] = (in_real * back[o, 0] + in_imag * back[o, 1]).astype(BF)
            grad_ref[1, i, o] = (in_real * back[o, 1] - in_imag * back[o, 0]).astype(BF)
        mixed[i, 0] = real
        mixed[i, 1] = imag
    modes_out(mixed, x_ref, y_back_ref, gather_ref, out_ref)
    for j in range(GX):
        out_ref[j, :, HI] = jnp.broadcast_to(sums_ref[...][None], (GY, 8, XY))


def tail_kernel(
    msg_ref, field_ref, cot_ref, mix_ref, bias_ref, perm_ref, pack_ref, inv_ref, back_ref, fold_ref,
    out_ref, grad_ref, coef_ref, sums_ref, flat, coef, back_coef, weight_sum,
):
    g = pl.program_id(0)
    block = field_ref.shape[1]

    @pl.when(g == 0)
    def _():
        unpack(msg_ref, perm_ref[...], 2 * CH, flat, coef)
        weight_sum[...] = jnp.zeros_like(weight_sum)

    total = jnp.zeros(weight_sum.shape, F32)
    for e in range(block):
        field = field_ref[:, e].reshape(CH * LY, ZT)
        left = coef[:, pl.ds(g * block + e, 1)].reshape(CH * LY, PAIRS)
        pre = dot(left, inv_ref[...]) + dot(mix_ref[...], field) + bias_ref[...]
        cot = cot_ref[:, e].reshape(CH * LY, ZT).astype(F32)
        square = pre * pre
        root = math.sqrt(2.0 / math.pi)
        bend = jnp.tanh(pre * (root + (root * 0.044715) * square))
        half = 0.5 + 0.5 * bend
        out_ref[:, e] = (pre * half).astype(BF).reshape(CH, LY, ZT)
        slope = half + (0.5 * pre) * ((1.0 - bend * bend) * (root + (3.0 * root * 0.044715) * square))
        grad = (cot * slope).astype(BF)
        grad_ref[:, e] = grad.reshape(CH, LY, ZT)
        back = dot(grad, back_ref[...]).astype(BF)
        back_coef[:, pl.ds(g * block + e, 1)] = back.reshape(CH, 1, LY, PAIRS)
        ones = jnp.concatenate([field, jnp.ones((16, ZT), BF)], 0)
        total += dot(ones, grad, ((1,), (1,)))
    weight_sum[...] += total

    @pl.when(g == pl.num_programs(0) - 1)
    def _():
        for ch in range(CH):
            flat[ch] = back_coef[ch].reshape(XY, PAIRS).T
        pack(flat, pack_ref[...], coef_ref)
        summed = weight_sum[...]
        rows = lax.broadcasted_iota(jnp.int32, summed.shape, 0)
        lanes = lax.broadcasted_iota(jnp.int32, summed.shape, 1)
        keep = (rows >= CH * LY) | (rows % LY == lanes % LY)
        by_row = jnp.where(keep, summed, 0.0)
        by_row = by_row.reshape(CH + 2, LY, CH * LY)
        by_row = jnp.concatenate(
            [jnp.sum(by_row[:CH], 1), by_row[CH, :1], jnp.zeros((3, CH * LY), F32)], 0
        )
        at = lax.broadcasted_iota(jnp.int32, (CH * LY, 128), 0) // LY
        to = lax.broadcasted_iota(jnp.int32, (CH * LY, 128), 1)
        gather = jnp.where(at == to, 1.0, 0.0)
        full = lax.dot_general(
            by_row, gather, (((1,), (0,)), ((), ())),
            precision=lax.Precision.HIGHEST, preferred_element_type=F32,
        )
        high = full.astype(BF)
        low = (full - high.astype(F32)).astype(BF)
        both = jnp.concatenate([high.astype(F32), low.astype(F32)], 0).astype(BF)
        folded = jnp.zeros((8, 128), F32)
        for s in range(6):
            folded += pltpu.roll(dot(fold_ref[s], both), CH * s, 1)
        sums_ref[...] = folded.astype(BF)


def last_kernel(
    msg_ref, grad_ref, mix_ref, perm_ref, table_ref, fold_ref, out_ref, sums_ref, flat, coef
):
    g = pl.program_id(0)
    block = grad_ref.shape[1]

    @pl.when(g == 0)
    def _():
        unpack(msg_ref, perm_ref[...], 48, flat, coef)
        summed = jnp.zeros((8, 128), F32)
        for m in range(MODES):
            summed += msg_ref[m * 48 + 40 : m * 48 + 48].astype(F32)
        lanes = lax.broadcasted_iota(jnp.int32, (8, 128), 1)
        full = jnp.zeros((48, 128), F32)
        for s in range(6):
            part = jnp.where(lanes < CH, pltpu.roll(summed, (128 - CH * s) % 128, 1), 0.0)
            full += lax.dot_general(
                fold_ref[s].astype(F32), part, (((0,), (0,)), ((), ())),
                precision=lax.Precision.HIGHEST, preferred_element_type=F32,
            )
        sums_ref[...] = (full[:24] + full[24:]) * (1.0 / math.sqrt(NX * NY * ZT))

    for e in range(block):
        left = coef[:, pl.ds(g * block + e, 1)].reshape(CH * LY, PAIRS)
        grad = grad_ref[:, e].reshape(CH * LY, ZT)
        total = dot(left, table_ref[...]) + dot(mix_ref[...], grad)
        out_ref[:, e] = total.astype(BF).reshape(CH, LY, ZT)


def exchange(messages):
    return lax.all_to_all(messages, AXES, split_axis=0, concat_axis=0, tiled=True)


def local(field, spectral_weight, bypass_weight, bypass_bias, cotangent):
    fwd_zt, inv_zt = plane_tables()
    x_parts = const(x_table())
    y_parts = const(y_table())
    y_back = const(y_table().T)
    spread = const(spread_table())
    gather = const(spread_table().T)
    perm = const(pack_table(40))
    perm_back = const(pack_table(40).T)
    perm_wide = const(pack_table(48).T)
    folds = const(fold_table())
    eye = jnp.eye(LY, dtype=BF)
    mix_in = jnp.kron(bypass_weight, eye)
    mix_out = jnp.kron(bypass_weight.T, eye)
    bias = jnp.repeat(bypass_bias, LY)[:, None]
    weight = spectral_weight.reshape(2, CH, CH, 8, 128)
    tiles = (GX, GY, HI, 8, XY)

    plane = plane_stage(field.reshape(CH, XY, ZT), const(fwd_zt), perm)
    arrived = exchange(plane.reshape(MODES, 2 * CH, XY))
    sent, spec = call(
        mix_kernel,
        (jax.ShapeDtypeStruct(tiles, BF), jax.ShapeDtypeStruct((CH, 2, 8, 128), F32)),
    )(arrived.reshape(tiles), weight, x_parts, y_parts, y_back, spread, gather)
    arrived = exchange(sent.reshape(MODES, 2 * CH, XY))

    block = 2
    cells = pl.BlockSpec((CH, block, LY, ZT), lambda g: (0, g, 0, 0))
    grid_shape = jax.ShapeDtypeStruct((CH, LX, LY, ZT), BF)
    out_field, grad_pre, back_coef, sums = call(
        tail_kernel,
        (
            grid_shape,
            grid_shape,
            jax.ShapeDtypeStruct((MODES * 2 * CH, XY), BF),
            jax.ShapeDtypeStruct((8, 128), BF),
        ),
        grid=(LX // block,),
        limit=56,
        in_specs=[
            whole((MODES * 2 * CH, XY)),
            cells,
            cells,
            whole((CH * LY, CH * LY)),
            whole((CH * LY, 1)),
            whole(perm.shape),
            whole(perm.shape),
            whole((PAIRS, ZT)),
            whole((ZT, PAIRS)),
            whole(folds.shape),
        ],
        out_specs=[cells, cells, whole((MODES * 2 * CH, XY)), whole((8, 128))],
        scratch_shapes=[
            pltpu.VMEM((CH, PAIRS, XY), BF),
            pltpu.VMEM((CH, LX, LY, PAIRS), BF),
            pltpu.VMEM((CH, LX, LY, PAIRS), BF),
            pltpu.VMEM((CH * LY + 16, CH * LY), F32),
        ],
    )(
        arrived.reshape(MODES * 2 * CH, XY), field, cotangent, mix_out, bias, perm_back, perm,
        const(inv_zt), const(inv_zt.T), folds,
    )

    arrived = exchange(back_coef.reshape(MODES, 2 * CH, XY))
    sent, spectral_grad = call(
        mix_back_kernel,
        (
            jax.ShapeDtypeStruct((GX, GY, HI + 1, 8, XY), BF),
            jax.ShapeDtypeStruct((2, CH, CH, 8, 128), BF),
        ),
    )(arrived.reshape(tiles), weight, spec, sums, x_parts, y_parts, y_back, spread, gather)
    arrived = exchange(sent.reshape(MODES, 48, XY))

    block = 4
    cells = pl.BlockSpec((CH, block, LY, ZT), lambda g: (0, g, 0, 0))
    field_grad, totals = call(
        last_kernel,
        (grid_shape, jax.ShapeDtypeStruct((24, 128), F32)),
        grid=(LX // block,),
        limit=56,
        in_specs=[
            whole((MODES * 48, XY)),
            cells,
            whole((CH * LY, CH * LY)),
            whole(perm_wide.shape),
            whole((PAIRS, ZT)),
            whole(folds.shape),
        ],
        out_specs=[cells, whole((24, 128))],
        scratch_shapes=[pltpu.VMEM((CH, PAIRS, XY), BF), pltpu.VMEM((CH, LX, LY, PAIRS), BF)],
    )(arrived.reshape(MODES * 48, XY), grad_pre, mix_in, perm_wide, const(fwd_zt.T), folds)
    spectral_grad = spectral_grad.reshape(spectral_weight.shape)
    return (out_field, field_grad, spectral_grad, totals[:CH, :CH], totals[CH, :CH])


def solution(mesh):
    in_specs = (
        P(None, "gx", "gy", None),
        P(None, AXES, None, None, None),
        P(),
        P(),
        P(None, "gx", "gy", None),
    )
    out_specs = (
        P(None, "gx", "gy", None),
        P(None, "gx", "gy", None),
        P(None, AXES, None, None, None),
        P(),
        P(),
    )
    return jax.shard_map(local, mesh=mesh, in_specs=in_specs, out_specs=out_specs, check_vma=False)
```

```python
import functools
import math

import jax
import jax.numpy as jnp
import ml_dtypes
import numpy as np
from jax import lax
from jax.experimental import pallas as pl
from jax.experimental.pallas import tpu as pltpu
from jax.sharding import PartitionSpec as P

NX = 128
NY = 128
NZ = 64
NT = 16
MX = 32
MY = 32
MZ = 16
MT = 8
CH = 20
GX = 8
GY = 16
LX = NX // GX
LY = NY // GY
XY = LX * LY
ZT = NZ * NT
PAIRS = 2 * MZ * MT
MODES = MZ * MT
HI = CH // 4
AXES = ("gx", "gy")
BF = jnp.bfloat16
F32 = jnp.float32
MIB = 1 << 20
LIMITS = (51, 51, 51, 51)
U = (8, 8, 5, 2)
LANES = 256


def mode_numbers(count):
    index = np.arange(count)
    return np.where(index < count // 2, index, index - count)


def plane_tables():
    z_freq = mode_numbers(MZ)
    t_freq = np.arange(MT)
    turn_z = (np.arange(NZ)[:, None] * z_freq[None, :] % NZ).astype(np.float32) / np.float32(NZ)
    turn_t = (np.arange(NT)[:, None] * t_freq[None, :] % NT).astype(np.float32) / np.float32(NT)
    angle = np.float32(2.0 * math.pi) * (turn_z[:, None, :, None] + turn_t[None, :, None, :])
    parts = np.stack([np.cos(angle), -np.sin(angle)], -1)
    factor = np.where(t_freq == 0, 1.0, 2.0).astype(np.float32)
    forward = parts.reshape(ZT, PAIRS) / np.float32(math.sqrt(ZT))
    inverse = (parts * factor[:, None]).reshape(ZT, PAIRS).T / np.float32(math.sqrt(PAIRS))
    return (forward.astype(ml_dtypes.bfloat16), inverse.astype(ml_dtypes.bfloat16))


def line_parts(length, kept):
    freqs = mode_numbers(kept)
    turns = (freqs[:, None] * np.arange(length)[None, :] % length).astype(np.float32)
    angle = np.float32(2.0 * math.pi / length) * turns
    norm = np.float32(math.sqrt(length))
    return (np.cos(angle) / norm, np.sin(angle) / norm)


def x_table():
    parts = np.stack(line_parts(NX, MX)).reshape(2, MX // 4, 4, GX, LX)
    table = np.einsum("phajw,vz->pvahjwz", parts, np.eye(LY, dtype=np.float32))
    return table.reshape(2 * LY * MX, GX * XY)


def y_table():
    cosine, sine = line_parts(NY, MY)
    block = np.stack(
        [
            np.stack([np.stack([cosine, -sine]), np.stack([sine, cosine])]),
            np.stack([np.stack([-sine, -cosine]), np.stack([cosine, -sine])]),
        ]
    )
    block = block.reshape(2, 2, 2, MY, GY, LY)
    table = np.einsum("sqpbkv,cd->svkcqdpb", block, np.eye(4, dtype=np.float32))
    return table.reshape(2 * LY * GY * 8, 8 * MY)


def spread_table():
    table = np.zeros((4, 4, MY, 4, 4, MY), np.float32)
    for low in range(4):
        for c in range(4):
            table[low, c, :, c, low, :] = np.eye(MY)
    return table.reshape(16 * MY, 16 * MY)


def pack_table(rows):
    table = np.zeros((8, rows, CH, 8, 2), np.float32)
    for m in range(8):
        for ch in range(CH):
            for r in range(2):
                table[m, 2 * ch + r, ch, m, r] = 1
    return table.reshape(8 * rows, CH * 16)


def fold_table():
    table = np.zeros((6, 8, 48), np.float32)
    for slot in range(42):
        table[slot % 6, slot // 6, slot if slot < 21 else slot + 3] = 1
    return table


def const(table):
    return jnp.asarray(np.asarray(table, np.float32).astype(ml_dtypes.bfloat16))


def dot(left, right, dims=((1,), (0,))):
    return lax.dot_general(left, right, (dims, ((), ())), preferred_element_type=F32)


def call(kernel, out, limit=28, cost=None, **kw):
    if cost is not None:
        cost = pl.CostEstimate(flops=cost[0], bytes_accessed=cost[1], transcendentals=0)
    return pl.pallas_call(
        kernel,
        out_shape=out,
        cost_estimate=cost,
        compiler_params=pltpu.CompilerParams(vmem_limit_bytes=int(limit * MIB)),
        **kw,
    )


VMEM = pl.BlockSpec(memory_space=pltpu.VMEM)
HBM = pl.BlockSpec(memory_space=pltpu.HBM)


def pack(coef, perm_ref, stage, out_ref, sems):
    def sent(b):
        rows = pl.ds(pl.multiple_of(b * 640, 640), 640)
        return pltpu.make_async_copy(stage.at[rows], out_ref.at[rows], sems.at[b])

    def step(b, carry):
        both = coef[:, pl.ds(pl.multiple_of(b * 32, 32), 32)]
        sides = [both[:, 16 * e : 16 * e + 16].reshape(16 * CH, XY) for e in range(2)]
        moved = dot(perm_ref[:, :320], jnp.concatenate(sides, 1)).astype(BF)
        for e in range(2):
            at = pl.multiple_of(b * 640 + e * 320, 320)
            stage[pl.ds(at, 320)] = moved[:, e * XY : (e + 1) * XY]
        sent(b).start()
        return carry

    def wait(b, carry):
        sent(b).wait()
        return carry

    lax.fori_loop(0, MODES // 16, step, 0, unroll=U[0])
    lax.fori_loop(0, MODES // 16, wait, 0, unroll=8)


def unpack(msg_ref, perm_ref, rows, flat, coef):
    def step(b, carry):
        sides = []
        for e in range(2):
            at = pl.multiple_of((2 * b + e) * 8 * rows, 8 * rows)
            sides.append(msg_ref[pl.ds(at, 8 * rows)])
        moved = dot(perm_ref[:, : 8 * rows], jnp.concatenate(sides, 1)).astype(BF)
        for e in range(2):
            part = moved[:, e * XY : (e + 1) * XY].reshape(CH, 16, XY)
            flat[:, pl.ds(pl.multiple_of(b * 32 + 16 * e, 16), 16)] = part
        return carry

    def turn(n, carry):
        for e in range(4):
            ch = n * 4 + e
            coef[pl.ds(ch, 1)] = flat[ch].T[None]
        return carry

    lax.fori_loop(0, MODES // 16, step, 0, unroll=U[1])
    lax.fori_loop(0, CH // 4, turn, 0, unroll=U[2])


def load(pairs, sems):
    moved = [pltpu.make_async_copy(s, t, sems.at[n]) for n, (s, t) in enumerate(pairs)]
    for copy in moved:
        copy.start()
    return moved


def first_kernel(
    field_hbm, table_hbm, perm_hbm, out_ref, field, table, perm, flat, stage, in_sems, field_sems, sems
):
    block = 4

    def part_copy(g):
        part = pl.ds(g * block, block)
        return pltpu.make_async_copy(field_hbm.at[part], field.at[part], field_sems.at[g])

    got = load([(table_hbm, table), (perm_hbm, perm)], in_sems)
    for g in range(CH // block):
        part_copy(g).start()
    got[0].wait()

    def step(g, carry):
        part_copy(g).wait()
        cells = field[pl.ds(g * block, block)].reshape(block * XY, ZT)
        coef = dot(cells, table[...]).astype(BF)
        for c in range(block):
            flat[pl.ds(g * block + c, 1)] = coef[c * XY : (c + 1) * XY].T[None]
        return carry

    lax.fori_loop(0, CH // block, step, 0)
    got[1].wait()
    pack(flat, perm, stage, out_ref, sems)


def plane_stage(field, table, perm):
    return call(
        first_kernel,
        jax.ShapeDtypeStruct((MODES * 2 * CH, XY), BF),
        limit=60,
        in_specs=[HBM] * 3,
        out_specs=HBM,
        scratch_shapes=[
            pltpu.VMEM((CH, XY, ZT), BF),
            pltpu.VMEM((ZT, PAIRS), BF),
            pltpu.VMEM(perm.shape, BF),
            pltpu.VMEM((CH, PAIRS, XY), BF),
            pltpu.VMEM((MODES * 2 * CH, XY), BF),
            pltpu.SemaphoreType.DMA((2,)),
            pltpu.SemaphoreType.DMA((5,)),
            pltpu.SemaphoreType.DMA((8,)),
        ],
    )(field, table, perm)


def mode_tables():
    tables = [x_table(), y_table(), y_table().T, spread_table(), spread_table().T]
    return np.concatenate(
        [t[:, c : c + 256] for t in tables for c in range(0, t.shape[1], 256)], 0
    )


def table_scratch():
    shapes = [(512, 1024), (2048, 256), (256, 2048), (512, 512), (512, 512)]
    return [pltpu.VMEM(shape, BF) for shape in shapes]


def table_pairs(tables_hbm, targets):
    groups = []
    row = 0
    for target in targets:
        group = []
        for c in range(0, target.shape[1], 256):
            rows = target.shape[0]
            group.append((tables_hbm.at[pl.ds(row, rows)], target.at[:, pl.ds(c, 256)]))
            row += rows
        groups.append(group)
    return groups


def tail_tables():
    inverse = plane_tables()[1].astype(np.float32)
    blocks = np.concatenate(np.split(inverse.T, 4), 1)
    perms = np.zeros((512, 1024), np.float32)
    perms[:320, :320] = pack_table(40).T
    perms[:320, 384:704] = pack_table(40)
    return np.concatenate([inverse, blocks, perms], 0)


def tail_pairs(tables_hbm, perm_ref, inv_ref, back_ref, pack_ref):
    perms = [(tables_hbm.at[pl.ds(512, 320), pl.ds(c, 384)], t) for c, t in ((0, perm_ref), (384, pack_ref))]
    blocks = [
        (tables_hbm.at[pl.ds(256, 256), pl.ds(256 * n, 256)], back_ref.at[pl.ds(256 * n, 256)])
        for n in range(4)
    ]
    return [perms[0], (tables_hbm.at[pl.ds(0, 256)], inv_ref)] + blocks + [perms[1]]


def last_tables():
    forward = plane_tables()[0].astype(np.float32).T
    folds = fold_table().reshape(48, 48)
    rest = np.zeros((768, 1024), np.float32)
    rest[:320, :384] = pack_table(48).T
    rest[320:368, :48] = folds
    return np.concatenate([forward, rest], 0)


def last_pairs(tables_hbm, perm_ref, table_ref, fold_ref):
    return [
        (tables_hbm.at[pl.ds(256, 320), pl.ds(0, 384)], perm_ref),
        (tables_hbm.at[pl.ds(0, 256)], table_ref),
        (tables_hbm.at[pl.ds(576, 48), pl.ds(0, 128)], fold_ref),
    ]


def ready(waits, n):
    for copy in waits[n]:
        copy.wait()


def modes_in(msg_ref, x_ref, y_ref, spread_ref, scale, waits):
    rows = [
        jnp.concatenate([msg_ref[j, :, hi].reshape(GY * 8, XY) for j in range(GX)], 1)
        for hi in range(HI)
    ]
    ready(waits, 0)
    after_x = dot(x_ref[...], jnp.concatenate(rows, 0), ((1,), (1,))).astype(BF)
    left = jnp.concatenate(
        [
            jnp.concatenate(
                [after_x[s * MX : (s + 1) * MX, hi * 128 : (hi + 1) * 128] for s in range(2 * LY)], 1
            )
            for hi in range(HI)
        ],
        0,
    )
    ready(waits, 1)
    after_y = dot(left, y_ref[...]) * scale
    grouped = jnp.concatenate(
        [
            jnp.concatenate(
                [
                    after_y[hi * MX + 8 * low : hi * MX + 8 * low + 8, t * 128 : (t + 1) * 128]
                    for low in range(4)
                ],
                1,
            )
            for t in range(2)
            for hi in range(HI)
        ],
        0,
    ).astype(BF)
    ready(waits, 3)
    spread = dot(grouped, spread_ref[...])
    found = {}
    for t in range(2):
        for hi in range(HI):
            for c in range(4):
                at = 4 * t + c
                row = (t * HI + hi) * 8
                found[hi * 4 + at // 2, at % 2] = spread[row : row + 8, c * 128 : (c + 1) * 128]
    return found


def modes_out(found, x_ref, y_back_ref, gather_ref, stage, out_ref, sems, waits):
    rows = []
    for t in range(2):
        for hi in range(HI):
            tiles = []
            for c in range(4):
                at = 4 * t + c
                tiles.append(found[hi * 4 + at // 2, at % 2])
            rows.append(jnp.concatenate(tiles, 1))
    ready(waits, 4)
    gathered = dot(jnp.concatenate(rows, 0).astype(BF), gather_ref[...])
    grouped = jnp.concatenate(
        [
            jnp.concatenate(
                [
                    gathered[(t * HI + hi) * 8 : (t * HI + hi) * 8 + 8, low * 128 : (low + 1) * 128]
                    for t in range(2)
                ],
                1,
            )
            for hi in range(HI)
            for low in range(4)
        ],
        0,
    ).astype(BF)
    ready(waits, 2)
    after_y = dot(grouped, y_back_ref[...]).astype(BF)
    left = jnp.concatenate(
        [
            jnp.concatenate(
                [
                    after_y[hi * MX : (hi + 1) * MX, s * 128 : (s + 1) * 128]
                    for hi in range(HI)
                ],
                1,
            )
            for s in range(2 * LY)
        ],
        0,
    )
    turned = left.T
    sent = []
    for j in range(0, GX, 2):
        after_x = dot(turned, x_ref[:, j * XY : (j + 2) * XY]).astype(BF)
        for e in range(2):
            for hi in range(HI):
                block = after_x[hi * 128 : (hi + 1) * 128, e * XY : (e + 1) * XY]
                stage[j + e, :, hi] = block.reshape(GY, 8, XY)
        part = pl.ds(j, 2)
        sent.append(pltpu.make_async_copy(stage.at[part], out_ref.at[part], sems.at[j // 2]))
        sent[-1].start()
    for copy in sent:
        copy.wait()


def mode_loads(tables_hbm, w_hbm, tables, w_ref, sems):
    groups = table_pairs(tables_hbm, tables)
    order = [groups[0], groups[1], groups[3], [(w_hbm, w_ref)], groups[4], groups[2]]
    moved = load([pair for group in order for pair in group], sems)
    split = []
    for group in order:
        split.append(moved[: len(group)])
        moved = moved[len(group) :]
    return [split[0], split[1], split[5], split[2], split[4]], split[3]


def mix_kernel(msg_ref, w_hbm, tables_hbm, out_ref, spec_ref, *scratch):
    x_ref, y_ref, y_back_ref, spread_ref, gather_ref, w_ref, stage, keep, mixed, in_sems, sems = scratch
    waits, weights = mode_loads(tables_hbm, w_hbm, scratch[:5], w_ref, in_sems)
    spec = modes_in(msg_ref, x_ref, y_ref, spread_ref, 1.0, waits)
    for i in range(CH):
        for r in range(2):
            keep[i, r] = spec[i, r]
    kept = pltpu.make_async_copy(keep, spec_ref.at[0], sems.at[4])
    kept.start()
    weights[0].wait()

    def step(o, carry):
        real = jnp.zeros((8, 128), F32)
        imag = jnp.zeros((8, 128), F32)
        for i in range(CH):
            w_real = w_ref[0, i, o].astype(F32)
            w_imag = w_ref[1, i, o].astype(F32)
            real += w_real * keep[i, 0] - w_imag * keep[i, 1]
            imag += w_real * keep[i, 1] + w_imag * keep[i, 0]
        mixed[o, 0] = 4.0 * real
        mixed[o, 1] = 4.0 * imag
        return carry

    lax.fori_loop(0, CH, step, 0)
    modes_out(mixed, x_ref, y_back_ref, gather_ref, stage, out_ref, sems, waits)
    kept.wait()


def mix_back_kernel(msg_ref, w_hbm, tables_hbm, sums_ref, out_ref, back_ref, *scratch):
    x_ref, y_ref, y_back_ref, spread_ref, gather_ref, w_ref, stage, keep, mixed, in_sems, sems = scratch
    waits, weights = mode_loads(tables_hbm, w_hbm, scratch[:5], w_ref, in_sems)
    for j in range(GX):
        stage[j, :, HI] = jnp.broadcast_to(sums_ref[...][None], (GY, 8, XY))
    back = modes_in(msg_ref, x_ref, y_ref, spread_ref, 4.0, waits)
    for i in range(CH):
        for r in range(2):
            keep[i, r] = back[i, r]
    kept = pltpu.make_async_copy(keep, back_ref.at[0], sems.at[4])
    kept.start()
    weights[0].wait()

    def step(i, carry):
        real = jnp.zeros((8, 128), F32)
        imag = jnp.zeros((8, 128), F32)
        for o in range(CH):
            w_real = w_ref[0, i, o].astype(F32)
            w_imag = w_ref[1, i, o].astype(F32)
            real += w_real * keep[o, 0] + w_imag * keep[o, 1]
            imag += w_real * keep[o, 1] - w_imag * keep[o, 0]
        mixed[i, 0] = real
        mixed[i, 1] = imag
        return carry

    lax.fori_loop(0, CH, step, 0)
    modes_out(mixed, x_ref, y_back_ref, gather_ref, stage, out_ref, sems, waits)
    kept.wait()


def outer_kernel(spec_hbm, back_hbm, grad_ref, spec_ref, back_ref, sems):
    for copy in load([(spec_hbm.at[0], spec_ref), (back_hbm.at[0], back_ref)], sems):
        copy.wait()

    def step(i, carry):
        in_real = spec_ref[i, 0]
        in_imag = spec_ref[i, 1]
        for o in range(CH):
            real = back_ref[o, 0]
            imag = back_ref[o, 1]
            grad_ref[0, i, o] = (in_real * real + in_imag * imag).astype(BF)
            grad_ref[1, i, o] = (in_real * imag - in_imag * real).astype(BF)
        return carry

    lax.fori_loop(0, CH, step, 0)


def bypass_kernel(after_hbm, cells_ref, mix_ref, bias_ref, out_ref):
    for e in range(cells_ref.shape[1]):
        cells = cells_ref[:, e].reshape(CH * LY, ZT)
        total = dot(mix_ref[...], cells) + bias_ref[...]
        out_ref[:, e] = total.reshape(CH, LY, ZT).astype(BF)


def tail_kernel(
    msg_ref, bypass_hbm, cot_hbm, tables_hbm, out_ref, grad_out_ref, coef_ref,
    bypass_ref, cot_ref, inv_ref, back_ref, perm_ref, pack_ref,
    flat, coef, back_coef, stage, out_stage, grad_ref,
    in_sems, bypass_sems, cot_sems, sems, grad_sems, coef_sems,
):
    cells = 16
    rows = CH * cells
    root = math.sqrt(2.0 / math.pi)
    got = load(tail_pairs(tables_hbm, perm_ref, inv_ref, back_ref, pack_ref), in_sems)

    def part(g):
        return pl.ds(pl.multiple_of(g * cells, cells), cells)

    def bypass_copy(g):
        return pltpu.make_async_copy(bypass_hbm.at[:, part(g)], bypass_ref.at[:, part(g)], bypass_sems.at[g])

    def cot_copy(g):
        return pltpu.make_async_copy(cot_hbm.at[:, part(g)], cot_ref.at[:, part(g)], cot_sems.at[g])

    def out_copy(g):
        return pltpu.make_async_copy(out_stage.at[g], out_ref.at[:, part(g)], sems.at[g])

    def grad_copy(g):
        return pltpu.make_async_copy(grad_ref.at[:, part(g)], grad_out_ref.at[:, part(g)], grad_sems.at[g])

    for g in range(XY // cells):
        bypass_copy(g).start()
        cot_copy(g).start()
    got[0].wait()
    unpack(msg_ref, perm_ref, 2 * CH, flat, coef)
    for copy in got[1:]:
        copy.wait()

    def step(g, carry):
        bypass_copy(g).wait()
        cot_copy(g).wait()
        left = coef[:, part(g)].reshape(rows, PAIRS)
        back = jnp.zeros((rows, PAIRS), F32)
        for z in range(0, ZT, LANES):
            at = slice(z, z + LANES)
            bypass = bypass_ref[:, part(g), at].reshape(rows, LANES).astype(F32)
            pre = dot(left, inv_ref[:, at]) + bypass
            cot = cot_ref[:, part(g), at].reshape(rows, LANES).astype(F32)
            square = pre * pre
            bend = jnp.tanh(pre * (root + (root * 0.044715) * square))
            half = 0.5 + 0.5 * bend
            out_stage[g, :, :, at] = (pre * half).astype(BF).reshape(CH, cells, LANES)
            rise = pre * (2.0 * root + (6.0 * root * 0.044715) * square)
            grad = (cot * (half * (1.0 + rise * (1.0 - half)))).astype(BF)
            grad_ref[:, part(g), at] = grad.reshape(CH, cells, LANES)
            back += dot(grad, back_ref[at])
        back_coef[:, part(g)] = back.astype(BF).reshape(CH, cells, PAIRS)
        out_copy(g).start()
        grad_copy(g).start()
        return carry

    def turn(n, carry):
        for e in range(4):
            ch = n * 4 + e
            flat[pl.ds(ch, 1)] = back_coef[ch].T[None]
        return carry

    def drain(g, carry):
        out_copy(g).wait()
        grad_copy(g).wait()
        return carry

    lax.fori_loop(0, XY // cells, step, 0, unroll=U[3])
    lax.fori_loop(0, CH // 4, turn, 0, unroll=U[2])
    pack(flat, pack_ref, stage, coef_ref, coef_sems)
    lax.fori_loop(0, XY // cells, drain, 0)


def sums_kernel(field_hbm, grad_hbm, fold_ref, sums_ref, field_ref, grad_ref, weight_sum, sems):
    for copy in load([(field_hbm, field_ref), (grad_hbm, grad_ref)], sems):
        copy.wait()
    weight_sum[...] = jnp.zeros_like(weight_sum)

    def step(u, carry):
        field = field_ref[:, pl.ds(u, 1)].reshape(CH * LY, ZT)
        grad = grad_ref[:, pl.ds(u, 1)].reshape(CH * LY, ZT)
        ones = jnp.concatenate([field, jnp.ones((16, ZT), BF)], 0)
        weight_sum[...] += dot(ones, grad, ((1,), (1,)))
        return carry

    lax.fori_loop(0, LX, step, 0)
    summed = weight_sum[...]
    rows = lax.broadcasted_iota(jnp.int32, summed.shape, 0)
    lanes = lax.broadcasted_iota(jnp.int32, summed.shape, 1)
    keep = (rows >= CH * LY) | (rows % LY == lanes % LY)
    by_row = jnp.where(keep, summed, 0.0).reshape(CH + 2, LY, CH * LY)
    by_row = jnp.concatenate(
        [jnp.sum(by_row[:CH], 1), by_row[CH, :1], jnp.zeros((3, CH * LY), F32)], 0
    )
    at = lax.broadcasted_iota(jnp.int32, (CH * LY, 128), 0) // LY
    to = lax.broadcasted_iota(jnp.int32, (CH * LY, 128), 1)
    gather = jnp.where(at == to, 1.0, 0.0)
    full = lax.dot_general(
        by_row, gather, (((1,), (0,)), ((), ())),
        precision=lax.Precision.HIGHEST, preferred_element_type=F32,
    )
    high = full.astype(BF)
    low = (full - high.astype(F32)).astype(BF)
    both = jnp.concatenate([high.astype(F32), low.astype(F32)], 0).astype(BF)
    folded = jnp.zeros((8, 128), F32)
    for s in range(6):
        folded += pltpu.roll(dot(fold_ref[s], both), CH * s, 1)
    sums_ref[...] = folded.astype(BF)


def last_kernel(
    msg_ref, bypass_hbm, tables_hbm, out_ref, weight_ref, bias_ref,
    bypass_ref, table_ref, perm_ref, fold_ref, flat, coef, out_stage, in_sems, bypass_sems, sems,
):
    cells = 16
    rows = CH * cells
    got = load(last_pairs(tables_hbm, perm_ref, table_ref, fold_ref), in_sems)

    def part(g):
        return pl.ds(pl.multiple_of(g * cells, cells), cells)

    def bypass_copy(g):
        return pltpu.make_async_copy(bypass_hbm.at[:, part(g)], bypass_ref.at[:, part(g)], bypass_sems.at[g])

    def out_copy(g):
        return pltpu.make_async_copy(out_stage.at[g], out_ref.at[:, part(g)], sems.at[g])

    for g in range(XY // cells):
        bypass_copy(g).start()
    got[0].wait()
    unpack(msg_ref, perm_ref, 48, flat, coef)
    for copy in got[1:]:
        copy.wait()

    def step(g, carry):
        bypass_copy(g).wait()
        left = coef[:, part(g)].reshape(rows, PAIRS)
        for z in range(0, ZT, LANES):
            at = slice(z, z + LANES)
            bypass = bypass_ref[:, part(g), at].reshape(rows, LANES).astype(F32)
            total = dot(left, table_ref[:, at]) + bypass
            out_stage[g, :, :, at] = total.astype(BF).reshape(CH, cells, LANES)
        out_copy(g).start()
        return carry

    lax.fori_loop(0, XY // cells, step, 0, unroll=U[3])

    def add(n, total):
        for e in range(8):
            at = pl.multiple_of((n * 8 + e) * 48 + 40, 8)
            total += msg_ref[pl.ds(at, 8)].astype(F32)
        return total

    summed = lax.fori_loop(0, MODES // 8, add, jnp.zeros((8, 128), F32))
    at = lax.broadcasted_iota(jnp.int32, (8, 128), 1)
    full = jnp.zeros((48, 128), F32)
    for s in range(6):
        own = jnp.where(at < CH, pltpu.roll(summed, (128 - CH * s) % 128, 1), 0.0)
        full += lax.dot_general(
            fold_ref[8 * s : 8 * s + 8, :48].astype(F32), own, (((0,), (0,)), ((), ())),
            precision=lax.Precision.HIGHEST, preferred_element_type=F32,
        )
    full = (full[:24] + full[24:]) * (1.0 / math.sqrt(NX * NY * ZT))
    weight_ref[...] = full[:CH, :CH]
    bias_ref[...] = full[CH : CH + 1, :CH]

    def drain(g, carry):
        out_copy(g).wait()
        return carry

    lax.fori_loop(0, XY // cells, drain, 0)


def exchange(messages):
    return lax.all_to_all(messages, AXES, split_axis=0, concat_axis=0, tiled=True)


DMA = pltpu.SemaphoreType.DMA
GRID = (CH, LX, LY, ZT)
MODE = (CH, 2, 8, 128)
TILES = (GX, GY, HI, 8, XY)
WIDE = (GX, GY, HI + 1, 8, XY)
MESSAGES = (MODES * 2 * CH, XY)
WEIGHT = (2, CH, CH, 8, 128)
MIX = (CH * LY, CH * LY)
FLOPS = 2 * CH * XY * ZT * PAIRS
FLAT = pltpu.VMEM((CH, PAIRS, XY), BF)
COEF = pltpu.VMEM((CH, XY, PAIRS), BF)
FLAT_GRID = (CH, XY, ZT)
CELLS = pltpu.VMEM(FLAT_GRID, BF)
OUT_STAGE = pltpu.VMEM((XY // 16, CH, 16, ZT), BF)
SLOTS = 13


def shaped(shape, kind=BF):
    return jax.ShapeDtypeStruct(shape, kind)


def mode_scratch(shape):
    kept = [pltpu.VMEM(WEIGHT, BF), pltpu.VMEM(shape, BF), pltpu.VMEM(MODE, F32), pltpu.VMEM(MODE, F32)]
    return table_scratch() + kept + [DMA((18,)), DMA((5,))]


def mix_stage(messages, weight, tables):
    return call(
        mix_kernel,
        (shaped(TILES), shaped((SLOTS, *MODE), F32)),
        limit=LIMITS[0],
        in_specs=[VMEM, HBM, HBM],
        out_specs=[HBM, HBM],
        scratch_shapes=mode_scratch(TILES),
    )(messages.reshape(TILES), weight, tables)


def bypass_stage(after, cells, mix, bias):
    block = pl.BlockSpec((CH, 2, LY, ZT), lambda g: (0, g, 0, 0))
    return call(
        bypass_kernel,
        shaped(GRID),
        limit=60,
        cost=(FLOPS, 2 * 5 * MIB),
        grid=(LX // 2,),
        in_specs=[HBM, block, pl.BlockSpec(MIX, lambda g: (0, 0)), pl.BlockSpec((CH * LY, 1), lambda g: (0, 0))],
        out_specs=block,
    )(after, cells, mix, bias).reshape(CH, XY, ZT)


def tail_stage(messages, bypass, cotangent, tables):
    perm = pltpu.VMEM((320, 384), BF)
    return call(
        tail_kernel,
        (shaped(FLAT_GRID), shaped(FLAT_GRID), shaped(MESSAGES)),
        limit=LIMITS[1],
        cost=(2 * FLOPS, 8 * 5 * MIB),
        in_specs=[VMEM] + [HBM] * 3,
        out_specs=[HBM, HBM, HBM],
        scratch_shapes=[
            CELLS, CELLS, pltpu.VMEM((PAIRS, ZT), BF), pltpu.VMEM((ZT, PAIRS), BF), perm, perm,
            FLAT, COEF, COEF, pltpu.VMEM(MESSAGES, BF), OUT_STAGE, CELLS,
            DMA((7,)), DMA((8,)), DMA((8,)), DMA((8,)), DMA((8,)), DMA((8,)),
        ],
    )(messages.reshape(MESSAGES), bypass, cotangent, tables)


def sums_stage(field, grad_pre, folds):
    return call(
        sums_kernel,
        shaped((8, 128)),
        limit=60,
        cost=(FLOPS, 2 * 5 * MIB),
        in_specs=[HBM, HBM, VMEM],
        out_specs=VMEM,
        scratch_shapes=[pltpu.VMEM(GRID, BF)] * 2 + [pltpu.VMEM((CH * LY + 16, CH * LY), F32), DMA((2,))],
    )(field, grad_pre, folds)


def mix_back_stage(messages, weight, tables, sums):
    return call(
        mix_back_kernel,
        (shaped(WIDE), shaped((SLOTS, *MODE), F32)),
        limit=LIMITS[2],
        in_specs=[VMEM, HBM, HBM, VMEM],
        out_specs=[HBM, HBM],
        scratch_shapes=mode_scratch(WIDE),
    )(messages.reshape(TILES), weight, tables, sums)


def outer_stage(spec, modes_back):
    return call(
        outer_kernel,
        shaped(WEIGHT),
        limit=60,
        cost=(8 * CH * CH * 1024, 2 * MIB),
        in_specs=[HBM, HBM],
        scratch_shapes=[pltpu.VMEM(MODE, F32), pltpu.VMEM(MODE, F32), DMA((2,))],
    )(spec, modes_back)


def last_stage(messages, bypass, tables):
    return call(
        last_kernel,
        (shaped(FLAT_GRID), shaped((CH, CH), F32), shaped((1, CH), F32)),
        limit=LIMITS[3],
        cost=(FLOPS, 2 * 5 * MIB),
        in_specs=[VMEM, HBM, HBM],
        out_specs=[HBM, VMEM, VMEM],
        scratch_shapes=[
            CELLS, pltpu.VMEM((PAIRS, ZT), BF), pltpu.VMEM((320, 384), BF), pltpu.VMEM((48, 128), BF),
            FLAT, COEF, OUT_STAGE, DMA((3,)), DMA((8,)), DMA((8,)),
        ],
    )(messages.reshape(MODES * 48, XY), bypass, tables)


def local(field, spectral_weight, bypass_weight, bypass_bias, cotangent):
    eye = jnp.eye(LY, dtype=BF)
    mix_in = jnp.kron(bypass_weight, eye)
    mix_out = jnp.kron(bypass_weight.T, eye)
    bias = jnp.repeat(bypass_bias, LY)[:, None]
    tables = const(mode_tables())
    weight = spectral_weight.reshape(WEIGHT)

    plane = plane_stage(field.reshape(FLAT_GRID), const(plane_tables()[0]), const(pack_table(40)))
    arrived = exchange(plane.reshape(MODES, 2 * CH, XY))
    bypass = bypass_stage(plane, field, mix_out, bias)
    sent, spec = mix_stage(arrived, weight, tables)
    arrived = exchange(sent.reshape(MODES, 2 * CH, XY))
    out_field, grad_pre, back_coef = tail_stage(
        arrived, bypass, cotangent.reshape(FLAT_GRID), const(tail_tables())
    )
    grad_pre = grad_pre.reshape(GRID)
    arrived = exchange(back_coef.reshape(MODES, 2 * CH, XY))
    sums = sums_stage(field, grad_pre, const(fold_table()))
    sent, modes_back = mix_back_stage(arrived, weight, tables, sums)
    arrived = exchange(sent.reshape(MODES, 48, XY))
    bypass = bypass_stage(back_coef, grad_pre, mix_in, jnp.zeros_like(bias))
    spectral_grad = outer_stage(spec, modes_back).reshape(spectral_weight.shape)
    field_grad, weight_grad, bias_grad = last_stage(arrived, bypass, const(last_tables()))
    return (
        out_field.reshape(GRID), field_grad.reshape(GRID), spectral_grad, weight_grad, bias_grad.reshape(CH),
    )


def solution(mesh):
    in_specs = (
        P(None, "gx", "gy", None),
        P(None, AXES, None, None, None),
        P(),
        P(),
        P(None, "gx", "gy", None),
    )
    out_specs = (
        P(None, "gx", "gy", None),
        P(None, "gx", "gy", None),
        P(None, AXES, None, None, None),
        P(),
        P(),
    )
    return jax.shard_map(local, mesh=mesh, in_specs=in_specs, out_specs=out_specs, check_vma=False)
```

```python
import functools
import math

import jax
import jax.numpy as jnp
import ml_dtypes
import numpy as np
from jax import lax
from jax.experimental import pallas as pl
from jax.experimental.pallas import tpu as pltpu
from jax.sharding import PartitionSpec as P

NX = 128
NY = 128
NZ = 64
NT = 16
MX = 32
MY = 32
MZ = 16
MT = 8
CH = 20
GX = 8
GY = 16
LX = NX // GX
LY = NY // GY
XY = LX * LY
ZT = NZ * NT
PAIRS = 2 * MZ * MT
MODES = MZ * MT
HI = CH // 4
AXES = ("gx", "gy")
BF = jnp.bfloat16
F32 = jnp.float32
MIB = 1 << 20
LIMITS = (51, 51, 51, 51)
U = (8, 8, 5, 2)
LANES = 256


def mode_numbers(count):
    index = np.arange(count)
    return np.where(index < count // 2, index, index - count)


def plane_tables():
    z_freq = mode_numbers(MZ)
    t_freq = np.arange(MT)
    turn_z = (np.arange(NZ)[:, None] * z_freq[None, :] % NZ).astype(np.float32) / np.float32(NZ)
    turn_t = (np.arange(NT)[:, None] * t_freq[None, :] % NT).astype(np.float32) / np.float32(NT)
    angle = np.float32(2.0 * math.pi) * (turn_z[:, None, :, None] + turn_t[None, :, None, :])
    parts = np.stack([np.cos(angle), -np.sin(angle)], -1)
    factor = np.where(t_freq == 0, 1.0, 2.0).astype(np.float32)
    forward = parts.reshape(ZT, PAIRS) / np.float32(math.sqrt(ZT))
    inverse = (parts * factor[:, None]).reshape(ZT, PAIRS).T / np.float32(math.sqrt(PAIRS))
    return (forward.astype(ml_dtypes.bfloat16), inverse.astype(ml_dtypes.bfloat16))


def line_parts(length, kept):
    freqs = mode_numbers(kept)
    turns = (freqs[:, None] * np.arange(length)[None, :] % length).astype(np.float32)
    angle = np.float32(2.0 * math.pi / length) * turns
    norm = np.float32(math.sqrt(length))
    return (np.cos(angle) / norm, np.sin(angle) / norm)


def x_table():
    parts = np.stack(line_parts(NX, MX)).reshape(2, MX // 4, 4, GX, LX)
    table = np.einsum("phajw,vz->pvahjwz", parts, np.eye(LY, dtype=np.float32))
    return table.reshape(2 * LY * MX, GX * XY)


def y_table():
    cosine, sine = line_parts(NY, MY)
    block = np.stack(
        [
            np.stack([np.stack([cosine, -sine]), np.stack([sine, cosine])]),
            np.stack([np.stack([-sine, -cosine]), np.stack([cosine, -sine])]),
        ]
    )
    block = block.reshape(2, 2, 2, MY, GY, LY)
    table = np.einsum("sqpbkv,cd->svkcqdpb", block, np.eye(4, dtype=np.float32))
    return table.reshape(2 * LY * GY * 8, 8 * MY)


def spread_table():
    table = np.zeros((4, 4, MY, 4, 4, MY), np.float32)
    for low in range(4):
        for c in range(4):
            table[low, c, :, c, low, :] = np.eye(MY)
    return table.reshape(16 * MY, 16 * MY)


def pack_table(rows):
    table = np.zeros((8, rows, CH, 8, 2), np.float32)
    for m in range(8):
        for ch in range(CH):
            for r in range(2):
                table[m, 2 * ch + r, ch, m, r] = 1
    return table.reshape(8 * rows, CH * 16)


def fold_table():
    table = np.zeros((6, 8, 48), np.float32)
    for slot in range(42):
        table[slot % 6, slot // 6, slot if slot < 21 else slot + 3] = 1
    return table


def const(table):
    return jnp.asarray(np.asarray(table, np.float32).astype(ml_dtypes.bfloat16))


def dot(left, right, dims=((1,), (0,))):
    return lax.dot_general(left, right, (dims, ((), ())), preferred_element_type=F32)


def call(kernel, out, limit=28, cost=None, **kw):
    if cost is not None:
        cost = pl.CostEstimate(flops=cost[0], bytes_accessed=cost[1], transcendentals=0)
    return pl.pallas_call(
        kernel,
        out_shape=out,
        cost_estimate=cost,
        compiler_params=pltpu.CompilerParams(vmem_limit_bytes=int(limit * MIB)),
        **kw,
    )


VMEM = pl.BlockSpec(memory_space=pltpu.VMEM)
HBM = pl.BlockSpec(memory_space=pltpu.HBM)


def pack(coef, perm_ref, stage, out_ref, sems):
    def sent(b):
        rows = pl.ds(pl.multiple_of(b * 640, 640), 640)
        return pltpu.make_async_copy(stage.at[rows], out_ref.at[rows], sems.at[b])

    def step(b, carry):
        both = coef[:, pl.ds(pl.multiple_of(b * 32, 32), 32)]
        sides = [both[:, 16 * e : 16 * e + 16].reshape(16 * CH, XY) for e in range(2)]
        moved = dot(perm_ref[:, :320], jnp.concatenate(sides, 1)).astype(BF)
        for e in range(2):
            at = pl.multiple_of(b * 640 + e * 320, 320)
            stage[pl.ds(at, 320)] = moved[:, e * XY : (e + 1) * XY]
        sent(b).start()
        return carry

    def wait(b, carry):
        sent(b).wait()
        return carry

    lax.fori_loop(0, MODES // 16, step, 0, unroll=U[0])
    lax.fori_loop(0, MODES // 16, wait, 0, unroll=8)


def unpack(msg_ref, perm_ref, rows, flat, coef):
    def step(b, carry):
        sides = []
        for e in range(2):
            at = pl.multiple_of((2 * b + e) * 8 * rows, 8 * rows)
            sides.append(msg_ref[pl.ds(at, 8 * rows)])
        moved = dot(perm_ref[:, : 8 * rows], jnp.concatenate(sides, 1)).astype(BF)
        for e in range(2):
            part = moved[:, e * XY : (e + 1) * XY].reshape(CH, 16, XY)
            flat[:, pl.ds(pl.multiple_of(b * 32 + 16 * e, 16), 16)] = part
        return carry

    def turn(n, carry):
        for e in range(4):
            ch = n * 4 + e
            coef[pl.ds(ch, 1)] = flat[ch].T[None]
        return carry

    lax.fori_loop(0, MODES // 16, step, 0, unroll=U[1])
    lax.fori_loop(0, CH // 4, turn, 0, unroll=U[2])


def load(pairs, sems):
    moved = [pltpu.make_async_copy(s, t, sems.at[n]) for n, (s, t) in enumerate(pairs)]
    for copy in moved:
        copy.start()
    return moved


def first_kernel(
    field_hbm, table_hbm, perm_hbm, out_ref, field, table, perm, flat, stage, in_sems, field_sems, sems
):
    block = 4

    def part_copy(g):
        part = pl.ds(g * block, block)
        return pltpu.make_async_copy(field_hbm.at[part], field.at[part], field_sems.at[g])

    got = load([(table_hbm, table), (perm_hbm, perm)], in_sems)
    for g in range(CH // block):
        part_copy(g).start()
    got[0].wait()

    def step(g, carry):
        part_copy(g).wait()
        cells = field[pl.ds(g * block, block)].reshape(block * XY, ZT)
        coef = dot(cells, table[...]).astype(BF)
        for c in range(block):
            flat[pl.ds(g * block + c, 1)] = coef[c * XY : (c + 1) * XY].T[None]
        return carry

    lax.fori_loop(0, CH // block, step, 0)
    got[1].wait()
    pack(flat, perm, stage, out_ref, sems)


def plane_stage(field, table, perm):
    return call(
        first_kernel,
        jax.ShapeDtypeStruct((MODES * 2 * CH, XY), BF),
        limit=60,
        in_specs=[HBM] * 3,
        out_specs=HBM,
        scratch_shapes=[
            pltpu.VMEM((CH, XY, ZT), BF),
            pltpu.VMEM((ZT, PAIRS), BF),
            pltpu.VMEM(perm.shape, BF),
            pltpu.VMEM((CH, PAIRS, XY), BF),
            pltpu.VMEM((MODES * 2 * CH, XY), BF),
            pltpu.SemaphoreType.DMA((2,)),
            pltpu.SemaphoreType.DMA((5,)),
            pltpu.SemaphoreType.DMA((8,)),
        ],
    )(field, table, perm)


def mode_tables():
    tables = [x_table(), y_table(), y_table().T, spread_table(), spread_table().T]
    return np.concatenate(
        [t[:, c : c + 256] for t in tables for c in range(0, t.shape[1], 256)], 0
    )


def table_scratch():
    shapes = [(512, 1024), (2048, 256), (256, 2048), (512, 512), (512, 512)]
    return [pltpu.VMEM(shape, BF) for shape in shapes]


def table_pairs(tables_hbm, targets):
    groups = []
    row = 0
    for target in targets:
        group = []
        for c in range(0, target.shape[1], 256):
            rows = target.shape[0]
            group.append((tables_hbm.at[pl.ds(row, rows)], target.at[:, pl.ds(c, 256)]))
            row += rows
        groups.append(group)
    return groups


def tail_tables():
    inverse = plane_tables()[1].astype(np.float32)
    blocks = np.concatenate(np.split(inverse.T, 4), 1)
    perms = np.zeros((512, 1024), np.float32)
    perms[:320, :320] = pack_table(40).T
    perms[:320, 384:704] = pack_table(40)
    return np.concatenate([inverse, blocks, perms], 0)


def tail_pairs(tables_hbm, perm_ref, inv_ref, back_ref, pack_ref):
    perms = [(tables_hbm.at[pl.ds(512, 320), pl.ds(c, 384)], t) for c, t in ((0, perm_ref), (384, pack_ref))]
    blocks = [
        (tables_hbm.at[pl.ds(256, 256), pl.ds(256 * n, 256)], back_ref.at[pl.ds(256 * n, 256)])
        for n in range(4)
    ]
    return [perms[0], (tables_hbm.at[pl.ds(0, 256)], inv_ref)] + blocks + [perms[1]]


def last_tables():
    forward = plane_tables()[0].astype(np.float32).T
    folds = fold_table().reshape(48, 48)
    rest = np.zeros((768, 1024), np.float32)
    rest[:320, :384] = pack_table(48).T
    rest[320:368, :48] = folds
    return np.concatenate([forward, rest], 0)


def last_pairs(tables_hbm, perm_ref, table_ref, fold_ref):
    return [
        (tables_hbm.at[pl.ds(256, 320), pl.ds(0, 384)], perm_ref),
        (tables_hbm.at[pl.ds(0, 256)], table_ref),
        (tables_hbm.at[pl.ds(576, 48), pl.ds(0, 128)], fold_ref),
    ]


def ready(waits, n):
    for copy in waits[n]:
        copy.wait()


def modes_in(msg_ref, x_ref, y_ref, spread_ref, scale, waits):
    rows = [
        jnp.concatenate([msg_ref[j, :, hi].reshape(GY * 8, XY) for j in range(GX)], 1)
        for hi in range(HI)
    ]
    ready(waits, 0)
    after_x = dot(x_ref[...], jnp.concatenate(rows, 0), ((1,), (1,))).astype(BF)
    left = jnp.concatenate(
        [
            jnp.concatenate(
                [after_x[s * MX : (s + 1) * MX, hi * 128 : (hi + 1) * 128] for s in range(2 * LY)], 1
            )
            for hi in range(HI)
        ],
        0,
    )
    ready(waits, 1)
    after_y = dot(left, y_ref[...]) * scale
    grouped = jnp.concatenate(
        [
            jnp.concatenate(
                [
                    after_y[hi * MX + 8 * low : hi * MX + 8 * low + 8, t * 128 : (t + 1) * 128]
                    for low in range(4)
                ],
                1,
            )
            for t in range(2)
            for hi in range(HI)
        ],
        0,
    ).astype(BF)
    ready(waits, 3)
    spread = dot(grouped, spread_ref[...])
    found = {}
    for t in range(2):
        for hi in range(HI):
            for c in range(4):
                at = 4 * t + c
                row = (t * HI + hi) * 8
                found[hi * 4 + at // 2, at % 2] = spread[row : row + 8, c * 128 : (c + 1) * 128]
    return found


def modes_out(found, x_ref, y_back_ref, gather_ref, stage, out_ref, sems, waits):
    rows = []
    for t in range(2):
        for hi in range(HI):
            tiles = []
            for c in range(4):
                at = 4 * t + c
                tiles.append(found[hi * 4 + at // 2, at % 2])
            rows.append(jnp.concatenate(tiles, 1))
    ready(waits, 4)
    gathered = dot(jnp.concatenate(rows, 0).astype(BF), gather_ref[...])
    grouped = jnp.concatenate(
        [
            jnp.concatenate(
                [
                    gathered[(t * HI + hi) * 8 : (t * HI + hi) * 8 + 8, low * 128 : (low + 1) * 128]
                    for t in range(2)
                ],
                1,
            )
            for hi in range(HI)
            for low in range(4)
        ],
        0,
    ).astype(BF)
    ready(waits, 2)
    after_y = dot(grouped, y_back_ref[...]).astype(BF)
    left = jnp.concatenate(
        [
            jnp.concatenate(
                [
                    after_y[hi * MX : (hi + 1) * MX, s * 128 : (s + 1) * 128]
                    for hi in range(HI)
                ],
                1,
            )
            for s in range(2 * LY)
        ],
        0,
    )
    turned = left.T
    sent = []
    for j in range(0, GX, 2):
        after_x = dot(turned, x_ref[:, j * XY : (j + 2) * XY]).astype(BF)
        for e in range(2):
            for hi in range(HI):
                block = after_x[hi * 128 : (hi + 1) * 128, e * XY : (e + 1) * XY]
                stage[j + e, :, hi] = block.reshape(GY, 8, XY)
        part = pl.ds(j, 2)
        sent.append(pltpu.make_async_copy(stage.at[part], out_ref.at[part], sems.at[j // 2]))
        sent[-1].start()
    for copy in sent:
        copy.wait()


def mode_loads(tables_hbm, w_hbm, tables, w_ref, sems):
    groups = table_pairs(tables_hbm, tables)
    order = [groups[0], groups[1], groups[3], [(w_hbm, w_ref)], groups[4], groups[2]]
    moved = load([pair for group in order for pair in group], sems)
    split = []
    for group in order:
        split.append(moved[: len(group)])
        moved = moved[len(group) :]
    return [split[0], split[1], split[5], split[2], split[4]], split[3]


def mix_kernel(msg_ref, w_hbm, tables_hbm, out_ref, spec_ref, *scratch):
    x_ref, y_ref, y_back_ref, spread_ref, gather_ref, w_ref, stage, keep, mixed, unused, in_sems, sems = scratch
    waits, weights = mode_loads(tables_hbm, w_hbm, scratch[:5], w_ref, in_sems)
    spec = modes_in(msg_ref, x_ref, y_ref, spread_ref, 1.0, waits)
    for i in range(CH):
        for r in range(2):
            keep[i, r] = spec[i, r]
    kept = pltpu.make_async_copy(keep, spec_ref.at[0], sems.at[4])
    kept.start()
    weights[0].wait()

    def step(o, carry):
        real = jnp.zeros((8, 128), F32)
        imag = jnp.zeros((8, 128), F32)
        for i in range(CH):
            w_real = w_ref[0, i, o].astype(F32)
            w_imag = w_ref[1, i, o].astype(F32)
            real += w_real * keep[i, 0] - w_imag * keep[i, 1]
            imag += w_real * keep[i, 1] + w_imag * keep[i, 0]
        mixed[o, 0] = 4.0 * real
        mixed[o, 1] = 4.0 * imag
        return carry

    lax.fori_loop(0, CH, step, 0)
    modes_out(mixed, x_ref, y_back_ref, gather_ref, stage, out_ref, sems, waits)
    kept.wait()


def mix_back_kernel(msg_ref, w_hbm, tables_hbm, sums_hbm, out_ref, back_ref, *scratch):
    x_ref, y_ref, y_back_ref, spread_ref, gather_ref, w_ref, stage, keep, mixed, sums_ref, in_sems, sems = scratch
    waits, weights = mode_loads(tables_hbm, w_hbm, scratch[:5], w_ref, in_sems)
    fetched = pltpu.make_async_copy(sums_hbm.at[0], sums_ref, sems.at[5])
    fetched.start()
    back = modes_in(msg_ref, x_ref, y_ref, spread_ref, 4.0, waits)
    fetched.wait()
    for j in range(GX):
        stage[j, :, HI] = jnp.broadcast_to(sums_ref[...][None], (GY, 8, XY))
    for i in range(CH):
        for r in range(2):
            keep[i, r] = back[i, r]
    kept = pltpu.make_async_copy(keep, back_ref.at[0], sems.at[4])
    kept.start()
    weights[0].wait()

    def step(i, carry):
        real = jnp.zeros((8, 128), F32)
        imag = jnp.zeros((8, 128), F32)
        for o in range(CH):
            w_real = w_ref[0, i, o].astype(F32)
            w_imag = w_ref[1, i, o].astype(F32)
            real += w_real * keep[o, 0] + w_imag * keep[o, 1]
            imag += w_real * keep[o, 1] - w_imag * keep[o, 0]
        mixed[i, 0] = real
        mixed[i, 1] = imag
        return carry

    lax.fori_loop(0, CH, step, 0)
    modes_out(mixed, x_ref, y_back_ref, gather_ref, stage, out_ref, sems, waits)
    kept.wait()


def outer_kernel(spec_hbm, back_hbm, grad_ref, spec_ref, back_ref, sems):
    for copy in load([(spec_hbm.at[0], spec_ref), (back_hbm.at[0], back_ref)], sems):
        copy.wait()

    def step(i, carry):
        in_real = spec_ref[i, 0]
        in_imag = spec_ref[i, 1]
        for o in range(CH):
            real = back_ref[o, 0]
            imag = back_ref[o, 1]
            grad_ref[0, i, o] = (in_real * real + in_imag * imag).astype(BF)
            grad_ref[1, i, o] = (in_real * imag - in_imag * real).astype(BF)
        return carry

    lax.fori_loop(0, CH, step, 0)


def bypass_kernel(after_hbm, cells_ref, mix_ref, bias_ref, out_ref):
    for e in range(cells_ref.shape[1]):
        cells = cells_ref[:, e].reshape(CH * LY, ZT)
        total = dot(mix_ref[...], cells) + bias_ref[...]
        out_ref[:, e] = total.reshape(CH, LY, ZT).astype(BF)


def tail_kernel(
    msg_ref, bypass_hbm, cot_hbm, tables_hbm, out_ref, grad_out_ref, coef_ref,
    bypass_ref, cot_ref, inv_ref, back_ref, perm_ref, pack_ref,
    flat, coef, back_coef, stage, out_stage, grad_ref,
    in_sems, bypass_sems, cot_sems, sems, grad_sems, coef_sems,
):
    cells = 16
    rows = CH * cells
    root = math.sqrt(2.0 / math.pi)
    got = load(tail_pairs(tables_hbm, perm_ref, inv_ref, back_ref, pack_ref), in_sems)

    def part(g):
        return pl.ds(pl.multiple_of(g * cells, cells), cells)

    def bypass_copy(g):
        return pltpu.make_async_copy(bypass_hbm.at[:, part(g)], bypass_ref.at[:, part(g)], bypass_sems.at[g])

    def cot_copy(g):
        return pltpu.make_async_copy(cot_hbm.at[:, part(g)], cot_ref.at[:, part(g)], cot_sems.at[g])

    def out_copy(g):
        return pltpu.make_async_copy(out_stage.at[g], out_ref.at[:, part(g)], sems.at[g])

    def grad_copy(g):
        return pltpu.make_async_copy(grad_ref.at[:, part(g)], grad_out_ref.at[:, part(g)], grad_sems.at[g])

    for g in range(XY // cells):
        bypass_copy(g).start()
        cot_copy(g).start()
    got[0].wait()
    unpack(msg_ref, perm_ref, 2 * CH, flat, coef)
    for copy in got[1:]:
        copy.wait()

    def step(g, carry):
        bypass_copy(g).wait()
        cot_copy(g).wait()
        left = coef[:, part(g)].reshape(rows, PAIRS)
        back = jnp.zeros((rows, PAIRS), F32)
        for z in range(0, ZT, LANES):
            at = slice(z, z + LANES)
            bypass = bypass_ref[:, part(g), at].reshape(rows, LANES).astype(F32)
            pre = dot(left, inv_ref[:, at]) + bypass
            cot = cot_ref[:, part(g), at].reshape(rows, LANES)
            square = pre * pre
            bend = jnp.tanh(pre * (root + (root * 0.044715) * square))
            half = 0.5 + 0.5 * bend
            out_stage[g, :, :, at] = (pre * half).astype(BF).reshape(CH, cells, LANES)
            half = half.astype(BF)
            near = pre.astype(BF)
            rise = near * (BF(2.0 * root) + BF(6.0 * root * 0.044715) * (near * near))
            grad = cot * (half * (BF(1.0) + rise * (BF(1.0) - half)))
            grad_ref[:, part(g), at] = grad.reshape(CH, cells, LANES)
            back += dot(grad, back_ref[at])
        back_coef[:, part(g)] = back.astype(BF).reshape(CH, cells, PAIRS)
        out_copy(g).start()
        grad_copy(g).start()
        return carry

    def turn(n, carry):
        for e in range(4):
            ch = n * 4 + e
            flat[pl.ds(ch, 1)] = back_coef[ch].T[None]
        return carry

    def drain(g, carry):
        out_copy(g).wait()
        grad_copy(g).wait()
        return carry

    lax.fori_loop(0, XY // cells, step, 0, unroll=U[3])
    lax.fori_loop(0, CH // 4, turn, 0, unroll=U[2])
    pack(flat, pack_ref, stage, coef_ref, coef_sems)
    lax.fori_loop(0, XY // cells, drain, 0)


def sums_kernel(
    field_hbm, grad_hbm, fold_ref, sums_ref, field_ref, grad_ref, weight_sum, folds_ref, sems
):
    for copy in load([(field_hbm, field_ref), (grad_hbm, grad_ref)], sems):
        copy.wait()
    weight_sum[...] = jnp.zeros_like(weight_sum)

    def step(u, carry):
        field = field_ref[:, pl.ds(u, 1)].reshape(CH * LY, ZT)
        grad = grad_ref[:, pl.ds(u, 1)].reshape(CH * LY, ZT)
        ones = jnp.concatenate([field, jnp.ones((16, ZT), BF)], 0)
        weight_sum[...] += dot(ones, grad, ((1,), (1,)))
        return carry

    lax.fori_loop(0, LX, step, 0)
    summed = weight_sum[...]
    rows = lax.broadcasted_iota(jnp.int32, summed.shape, 0)
    lanes = lax.broadcasted_iota(jnp.int32, summed.shape, 1)
    keep = (rows >= CH * LY) | (rows % LY == lanes % LY)
    by_row = jnp.where(keep, summed, 0.0).reshape(CH + 2, LY, CH * LY)
    by_row = jnp.concatenate(
        [jnp.sum(by_row[:CH], 1), by_row[CH, :1], jnp.zeros((3, CH * LY), F32)], 0
    )
    at = lax.broadcasted_iota(jnp.int32, (CH * LY, 128), 0) // LY
    to = lax.broadcasted_iota(jnp.int32, (CH * LY, 128), 1)
    gather = jnp.where(at == to, 1.0, 0.0)
    full = lax.dot_general(
        by_row, gather, (((1,), (0,)), ((), ())),
        precision=lax.Precision.HIGHEST, preferred_element_type=F32,
    )
    high = full.astype(BF)
    low = (full - high.astype(F32)).astype(BF)
    both = jnp.concatenate([high.astype(F32), low.astype(F32)], 0).astype(BF)
    folded = jnp.zeros((8, 128), F32)
    for s in range(6):
        folded += pltpu.roll(dot(fold_ref[s], both), CH * s, 1)
    folds_ref[...] = folded.astype(BF)
    sent = pltpu.make_async_copy(folds_ref, sums_ref.at[0], sems.at[0])
    sent.start()
    sent.wait()


def last_kernel(
    msg_ref, bypass_hbm, tables_hbm, out_ref, weight_ref, bias_ref,
    bypass_ref, table_ref, perm_ref, fold_ref, flat, coef, out_stage, in_sems, bypass_sems, sems,
):
    cells = 16
    rows = CH * cells
    got = load(last_pairs(tables_hbm, perm_ref, table_ref, fold_ref), in_sems)

    def part(g):
        return pl.ds(pl.multiple_of(g * cells, cells), cells)

    def bypass_copy(g):
        return pltpu.make_async_copy(bypass_hbm.at[:, part(g)], bypass_ref.at[:, part(g)], bypass_sems.at[g])

    def out_copy(g):
        return pltpu.make_async_copy(out_stage.at[g], out_ref.at[:, part(g)], sems.at[g])

    for g in range(XY // cells):
        bypass_copy(g).start()
    got[0].wait()
    unpack(msg_ref, perm_ref, 48, flat, coef)
    for copy in got[1:]:
        copy.wait()

    def step(g, carry):
        bypass_copy(g).wait()
        left = coef[:, part(g)].reshape(rows, PAIRS)
        for z in range(0, ZT, LANES):
            at = slice(z, z + LANES)
            bypass = bypass_ref[:, part(g), at].reshape(rows, LANES).astype(F32)
            total = dot(left, table_ref[:, at]) + bypass
            out_stage[g, :, :, at] = total.astype(BF).reshape(CH, cells, LANES)
        out_copy(g).start()
        return carry

    lax.fori_loop(0, XY // cells, step, 0, unroll=U[3])

    def add(n, total):
        for e in range(8):
            at = pl.multiple_of((n * 8 + e) * 48 + 40, 8)
            total += msg_ref[pl.ds(at, 8)].astype(F32)
        return total

    summed = lax.fori_loop(0, MODES // 8, add, jnp.zeros((8, 128), F32))
    at = lax.broadcasted_iota(jnp.int32, (8, 128), 1)
    full = jnp.zeros((48, 128), F32)
    for s in range(6):
        own = jnp.where(at < CH, pltpu.roll(summed, (128 - CH * s) % 128, 1), 0.0)
        full += lax.dot_general(
            fold_ref[8 * s : 8 * s + 8, :48].astype(F32), own, (((0,), (0,)), ((), ())),
            precision=lax.Precision.HIGHEST, preferred_element_type=F32,
        )
    full = (full[:24] + full[24:]) * (1.0 / math.sqrt(NX * NY * ZT))
    weight_ref[...] = full[:CH, :CH]
    bias_ref[...] = full[CH : CH + 1, :CH]

    def drain(g, carry):
        out_copy(g).wait()
        return carry

    lax.fori_loop(0, XY // cells, drain, 0)


def exchange(messages):
    return lax.all_to_all(messages, AXES, split_axis=0, concat_axis=0, tiled=True)


DMA = pltpu.SemaphoreType.DMA
GRID = (CH, LX, LY, ZT)
MODE = (CH, 2, 8, 128)
TILES = (GX, GY, HI, 8, XY)
WIDE = (GX, GY, HI + 1, 8, XY)
MESSAGES = (MODES * 2 * CH, XY)
WEIGHT = (2, CH, CH, 8, 128)
MIX = (CH * LY, CH * LY)
FLOPS = 2 * CH * XY * ZT * PAIRS
FLAT = pltpu.VMEM((CH, PAIRS, XY), BF)
COEF = pltpu.VMEM((CH, XY, PAIRS), BF)
FLAT_GRID = (CH, XY, ZT)
CELLS = pltpu.VMEM(FLAT_GRID, BF)
OUT_STAGE = pltpu.VMEM((XY // 16, CH, 16, ZT), BF)
SLOTS = 13


def shaped(shape, kind=BF):
    return jax.ShapeDtypeStruct(shape, kind)


def mode_scratch(shape):
    kept = [pltpu.VMEM(WEIGHT, BF), pltpu.VMEM(shape, BF), pltpu.VMEM(MODE, F32), pltpu.VMEM(MODE, F32)]
    return table_scratch() + kept + [pltpu.VMEM((8, 128), BF), DMA((18,)), DMA((6,))]


def mix_stage(messages, weight, tables):
    return call(
        mix_kernel,
        (shaped(TILES), shaped((SLOTS, *MODE), F32)),
        limit=LIMITS[0],
        in_specs=[VMEM, HBM, HBM],
        out_specs=[HBM, HBM],
        scratch_shapes=mode_scratch(TILES),
    )(messages.reshape(TILES), weight, tables)


def bypass_stage(after, cells, mix, bias):
    block = pl.BlockSpec((CH, 2, LY, ZT), lambda g: (0, g, 0, 0))
    return call(
        bypass_kernel,
        shaped(GRID),
        limit=60,
        cost=(FLOPS, 2 * 5 * MIB),
        grid=(LX // 2,),
        in_specs=[HBM, block, pl.BlockSpec(MIX, lambda g: (0, 0)), pl.BlockSpec((CH * LY, 1), lambda g: (0, 0))],
        out_specs=block,
    )(after, cells, mix, bias).reshape(CH, XY, ZT)


def tail_stage(messages, bypass, cotangent, tables):
    perm = pltpu.VMEM((320, 384), BF)
    return call(
        tail_kernel,
        (shaped(FLAT_GRID), shaped(FLAT_GRID), shaped(MESSAGES)),
        limit=LIMITS[1],
        cost=(2 * FLOPS, 8 * 5 * MIB),
        in_specs=[VMEM] + [HBM] * 3,
        out_specs=[HBM, HBM, HBM],
        scratch_shapes=[
            CELLS, CELLS, pltpu.VMEM((PAIRS, ZT), BF), pltpu.VMEM((ZT, PAIRS), BF), perm, perm,
            FLAT, COEF, COEF, pltpu.VMEM(MESSAGES, BF), OUT_STAGE, CELLS,
            DMA((7,)), DMA((8,)), DMA((8,)), DMA((8,)), DMA((8,)), DMA((8,)),
        ],
    )(messages.reshape(MESSAGES), bypass, cotangent, tables)


def sums_stage(field, grad_pre, folds):
    return call(
        sums_kernel,
        shaped((1280, 8, 128)),
        limit=60,
        cost=(FLOPS, 2 * 5 * MIB),
        in_specs=[HBM, HBM, VMEM],
        out_specs=HBM,
        scratch_shapes=[pltpu.VMEM(GRID, BF)] * 2
        + [pltpu.VMEM((CH * LY + 16, CH * LY), F32), pltpu.VMEM((8, 128), BF), DMA((2,))],
    )(field, grad_pre, folds)


def mix_back_stage(messages, weight, tables, sums):
    return call(
        mix_back_kernel,
        (shaped(WIDE), shaped((SLOTS, *MODE), F32)),
        limit=LIMITS[2],
        in_specs=[VMEM, HBM, HBM, HBM],
        out_specs=[HBM, HBM],
        scratch_shapes=mode_scratch(WIDE),
    )(messages.reshape(TILES), weight, tables, sums)


def outer_stage(spec, modes_back):
    return call(
        outer_kernel,
        shaped(WEIGHT),
        limit=60,
        cost=(8 * CH * CH * 1024, 2 * MIB),
        in_specs=[HBM, HBM],
        scratch_shapes=[pltpu.VMEM(MODE, F32), pltpu.VMEM(MODE, F32), DMA((2,))],
    )(spec, modes_back)


def last_stage(messages, bypass, tables):
    return call(
        last_kernel,
        (shaped(FLAT_GRID), shaped((CH, CH), F32), shaped((1, CH), F32)),
        limit=LIMITS[3],
        cost=(FLOPS, 2 * 5 * MIB),
        in_specs=[VMEM, HBM, HBM],
        out_specs=[HBM, VMEM, VMEM],
        scratch_shapes=[
            CELLS, pltpu.VMEM((PAIRS, ZT), BF), pltpu.VMEM((320, 384), BF), pltpu.VMEM((48, 128), BF),
            FLAT, COEF, OUT_STAGE, DMA((3,)), DMA((8,)), DMA((8,)),
        ],
    )(messages.reshape(MODES * 48, XY), bypass, tables)


def local(field, spectral_weight, bypass_weight, bypass_bias, cotangent):
    eye = jnp.eye(LY, dtype=BF)
    mix_in = jnp.kron(bypass_weight, eye)
    mix_out = jnp.kron(bypass_weight.T, eye)
    bias = jnp.repeat(bypass_bias, LY)[:, None]
    tables = const(mode_tables())
    weight = spectral_weight.reshape(WEIGHT)

    plane = plane_stage(field.reshape(FLAT_GRID), const(plane_tables()[0]), const(pack_table(40)))
    arrived = exchange(plane.reshape(MODES, 2 * CH, XY))
    bypass = bypass_stage(plane, field, mix_out, bias)
    sent, spec = mix_stage(arrived, weight, tables)
    arrived = exchange(sent.reshape(MODES, 2 * CH, XY))
    out_field, grad_pre, back_coef = tail_stage(
        arrived, bypass, cotangent.reshape(FLAT_GRID), const(tail_tables())
    )
    grad_pre = grad_pre.reshape(GRID)
    arrived = exchange(back_coef.reshape(MODES, 2 * CH, XY))
    sums = sums_stage(field, grad_pre, const(fold_table()))
    sent, modes_back = mix_back_stage(arrived, weight, tables, sums)
    arrived = exchange(sent.reshape(MODES, 48, XY))
    bypass = bypass_stage(back_coef, grad_pre, mix_in, jnp.zeros_like(bias))
    spectral_grad = outer_stage(spec, modes_back).reshape(spectral_weight.shape)
    field_grad, weight_grad, bias_grad = last_stage(arrived, bypass, const(last_tables()))
    return (
        out_field.reshape(GRID), field_grad.reshape(GRID), spectral_grad, weight_grad, bias_grad.reshape(CH),
    )


def solution(mesh):
    in_specs = (
        P(None, "gx", "gy", None),
        P(None, AXES, None, None, None),
        P(),
        P(),
        P(None, "gx", "gy", None),
    )
    out_specs = (
        P(None, "gx", "gy", None),
        P(None, "gx", "gy", None),
        P(None, AXES, None, None, None),
        P(),
        P(),
    )
    return jax.shard_map(local, mesh=mesh, in_specs=in_specs, out_specs=out_specs, check_vma=False)
```

```python
import functools
import math

import jax
import jax.numpy as jnp
import ml_dtypes
import numpy as np
from jax import lax
from jax.experimental import pallas as pl
from jax.experimental.pallas import tpu as pltpu
from jax.sharding import PartitionSpec as P

NX = 128
NY = 128
NZ = 64
NT = 16
MX = 32
MY = 32
MZ = 16
MT = 8
CH = 20
GX = 8
GY = 16
LX = NX // GX
LY = NY // GY
XY = LX * LY
ZT = NZ * NT
PAIRS = 2 * MZ * MT
MODES = MZ * MT
HI = CH // 4
AXES = ("gx", "gy")
BF = jnp.bfloat16
F32 = jnp.float32
MIB = 1 << 20
LIMITS = (51, 51, 51, 51)
U = (8, 8, 5, 2)
LANES = 256


def mode_numbers(count):
    index = np.arange(count)
    return np.where(index < count // 2, index, index - count)


def plane_tables():
    z_freq = mode_numbers(MZ)
    t_freq = np.arange(MT)
    turn_z = (np.arange(NZ)[:, None] * z_freq[None, :] % NZ).astype(np.float32) / np.float32(NZ)
    turn_t = (np.arange(NT)[:, None] * t_freq[None, :] % NT).astype(np.float32) / np.float32(NT)
    angle = np.float32(2.0 * math.pi) * (turn_z[:, None, :, None] + turn_t[None, :, None, :])
    parts = np.stack([np.cos(angle), -np.sin(angle)], -1)
    factor = np.where(t_freq == 0, 1.0, 2.0).astype(np.float32)
    forward = parts.reshape(ZT, PAIRS) / np.float32(math.sqrt(ZT))
    inverse = (parts * factor[:, None]).reshape(ZT, PAIRS).T / np.float32(math.sqrt(PAIRS))
    return (forward.astype(ml_dtypes.bfloat16), inverse.astype(ml_dtypes.bfloat16))


def line_parts(length, kept):
    freqs = mode_numbers(kept)
    turns = (freqs[:, None] * np.arange(length)[None, :] % length).astype(np.float32)
    angle = np.float32(2.0 * math.pi / length) * turns
    norm = np.float32(math.sqrt(length))
    return (np.cos(angle) / norm, np.sin(angle) / norm)


def x_table():
    parts = np.stack(line_parts(NX, MX)).reshape(2, MX // 4, 4, GX, LX)
    table = np.einsum("phajw,vz->pvahjwz", parts, np.eye(LY, dtype=np.float32))
    return table.reshape(2 * LY * MX, GX * XY)


def y_table():
    cosine, sine = line_parts(NY, MY)
    block = np.stack(
        [
            np.stack([np.stack([cosine, -sine]), np.stack([sine, cosine])]),
            np.stack([np.stack([-sine, -cosine]), np.stack([cosine, -sine])]),
        ]
    )
    block = block.reshape(2, 2, 2, MY, GY, LY)
    table = np.einsum("sqpbkv,cd->svkcqdpb", block, np.eye(4, dtype=np.float32))
    return table.reshape(2 * LY * GY * 8, 8 * MY)


def spread_table():
    table = np.zeros((4, 4, MY, 4, 4, MY), np.float32)
    for low in range(4):
        for c in range(4):
            table[low, c, :, c, low, :] = np.eye(MY)
    return table.reshape(16 * MY, 16 * MY)


def pack_table(rows):
    table = np.zeros((4, rows, CH, 4, 2), np.float32)
    for m in range(4):
        for ch in range(CH):
            for r in range(2):
                table[m, 2 * ch + r, ch, m, r] = 1
    return table.reshape(4 * rows, CH * 8)


def fold_table():
    table = np.zeros((6, 8, 48), np.float32)
    for slot in range(42):
        table[slot % 6, slot // 6, slot if slot < 21 else slot + 3] = 1
    return table


def const(table):
    return jnp.asarray(np.asarray(table, np.float32).astype(ml_dtypes.bfloat16))


def dot(left, right, dims=((1,), (0,))):
    return lax.dot_general(left, right, (dims, ((), ())), preferred_element_type=F32)


def call(kernel, out, limit=28, cost=None, **kw):
    if cost is not None:
        cost = pl.CostEstimate(flops=cost[0], bytes_accessed=cost[1], transcendentals=0)
    return pl.pallas_call(
        kernel,
        out_shape=out,
        cost_estimate=cost,
        compiler_params=pltpu.CompilerParams(vmem_limit_bytes=int(limit * MIB)),
        **kw,
    )


VMEM = pl.BlockSpec(memory_space=pltpu.VMEM)
HBM = pl.BlockSpec(memory_space=pltpu.HBM)


def pack(coef, perm_ref, stage, out_ref, sems):
    def sent(b):
        rows = pl.ds(pl.multiple_of(b * 640, 640), 640)
        return pltpu.make_async_copy(stage.at[rows], out_ref.at[rows], sems.at[b])

    def step(b, carry):
        for n in range(2):
            both = coef[:, pl.ds(pl.multiple_of(b * 32 + n * 16, 16), 16)].astype(F32)
            sides = [both[:, 8 * e : 8 * e + 8].reshape(8 * CH, XY).astype(BF) for e in range(2)]
            moved = dot(perm_ref[:160, :160], jnp.concatenate(sides, 1)).astype(BF)
            for e in range(2):
                at = pl.multiple_of(b * 640 + n * 320 + e * 160, 160)
                stage[pl.ds(at, 160)] = moved[:, e * XY : (e + 1) * XY]
        sent(b).start()
        return carry

    def wait(b, carry):
        sent(b).wait()
        return carry

    lax.fori_loop(0, MODES // 16, step, 0, unroll=U[0])
    lax.fori_loop(0, MODES // 16, wait, 0, unroll=8)


def unpack(msg_ref, perm_ref, rows, flat, coef):
    def step(b, carry):
        for n in range(2):
            sides = []
            for e in range(2):
                at = pl.multiple_of((4 * b + 2 * n + e) * 4 * rows, 4 * rows)
                sides.append(msg_ref[pl.ds(at, 4 * rows)])
            moved = dot(perm_ref[:160, : 4 * rows], jnp.concatenate(sides, 1))
            halves = [moved[:, e * XY : (e + 1) * XY].reshape(CH, 8, XY) for e in range(2)]
            part = jnp.concatenate(halves, 1).astype(BF)
            flat[:, pl.ds(pl.multiple_of(b * 32 + 16 * n, 16), 16)] = part
        return carry

    def turn(n, carry):
        for e in range(4):
            ch = n * 4 + e
            coef[pl.ds(ch, 1)] = flat[ch].T[None]
        return carry

    lax.fori_loop(0, MODES // 16, step, 0, unroll=U[1])
    lax.fori_loop(0, CH // 4, turn, 0, unroll=U[2])


def load(pairs, sems):
    moved = [pltpu.make_async_copy(s, t, sems.at[n]) for n, (s, t) in enumerate(pairs)]
    for copy in moved:
        copy.start()
    return moved


def first_kernel(
    field_hbm, table_hbm, perm_hbm, out_ref, field, table, perm, flat, stage, in_sems, field_sems, sems
):
    block = 4

    def part_copy(g):
        part = pl.ds(g * block, block)
        return pltpu.make_async_copy(field_hbm.at[part], field.at[part], field_sems.at[g])

    got = load([(table_hbm, table), (perm_hbm, perm)], in_sems)
    for g in range(CH // block):
        part_copy(g).start()
    got[0].wait()

    def step(g, carry):
        part_copy(g).wait()
        cells = field[pl.ds(g * block, block)].reshape(block * XY, ZT)
        coef = dot(cells, table[...]).astype(BF)
        for c in range(block):
            flat[pl.ds(g * block + c, 1)] = coef[c * XY : (c + 1) * XY].T[None]
        return carry

    lax.fori_loop(0, CH // block, step, 0)
    got[1].wait()
    pack(flat, perm, stage, out_ref, sems)


def plane_stage(field, table, perm):
    return call(
        first_kernel,
        jax.ShapeDtypeStruct((MODES * 2 * CH, XY), BF),
        limit=60,
        in_specs=[HBM] * 3,
        out_specs=HBM,
        scratch_shapes=[
            pltpu.VMEM((CH, XY, ZT), BF),
            pltpu.VMEM((ZT, PAIRS), BF),
            pltpu.VMEM(perm.shape, BF),
            pltpu.VMEM((CH, PAIRS, XY), BF),
            pltpu.VMEM((MODES * 2 * CH, XY), BF),
            pltpu.SemaphoreType.DMA((2,)),
            pltpu.SemaphoreType.DMA((5,)),
            pltpu.SemaphoreType.DMA((8,)),
        ],
    )(field, table, perm)


def mode_tables():
    tables = [x_table(), y_table(), y_table().T, spread_table(), spread_table().T]
    return np.concatenate(
        [t[:, c : c + 256] for t in tables for c in range(0, t.shape[1], 256)], 0
    )


def table_scratch():
    shapes = [(512, 1024), (2048, 256), (256, 2048), (512, 512), (512, 512)]
    return [pltpu.VMEM(shape, BF) for shape in shapes]


def table_pairs(tables_hbm, targets):
    groups = []
    row = 0
    for target in targets:
        group = []
        for c in range(0, target.shape[1], 256):
            rows = target.shape[0]
            group.append((tables_hbm.at[pl.ds(row, rows)], target.at[:, pl.ds(c, 256)]))
            row += rows
        groups.append(group)
    return groups


def tail_tables():
    inverse = plane_tables()[1].astype(np.float32)
    blocks = np.concatenate(np.split(inverse.T, 4), 1)
    perms = np.zeros((512, 1024), np.float32)
    perms[:160, :160] = pack_table(40).T
    perms[:160, 384:544] = pack_table(40)
    return np.concatenate([inverse, blocks, perms], 0)


def tail_pairs(tables_hbm, perm_ref, inv_ref, back_ref, pack_ref):
    perms = [(tables_hbm.at[pl.ds(512, 320), pl.ds(c, 384)], t) for c, t in ((0, perm_ref), (384, pack_ref))]
    blocks = [
        (tables_hbm.at[pl.ds(256, 256), pl.ds(256 * n, 256)], back_ref.at[pl.ds(256 * n, 256)])
        for n in range(4)
    ]
    return [perms[0], (tables_hbm.at[pl.ds(0, 256)], inv_ref)] + blocks + [perms[1]]


def last_tables():
    forward = plane_tables()[0].astype(np.float32).T
    folds = fold_table().reshape(48, 48)
    rest = np.zeros((768, 1024), np.float32)
    rest[:160, :192] = pack_table(48).T
    rest[320:368, :48] = folds
    return np.concatenate([forward, rest], 0)


def last_pairs(tables_hbm, perm_ref, table_ref, fold_ref):
    return [
        (tables_hbm.at[pl.ds(256, 320), pl.ds(0, 384)], perm_ref),
        (tables_hbm.at[pl.ds(0, 256)], table_ref),
        (tables_hbm.at[pl.ds(576, 48), pl.ds(0, 128)], fold_ref),
    ]


def ready(waits, n):
    for copy in waits[n]:
        copy.wait()


def modes_in(msg_ref, x_ref, y_ref, spread_ref, scale, waits):
    rows = [
        jnp.concatenate([msg_ref[j, :, hi].reshape(GY * 8, XY) for j in range(GX)], 1)
        for hi in range(HI)
    ]
    ready(waits, 0)
    after_x = dot(x_ref[...], jnp.concatenate(rows, 0), ((1,), (1,))).astype(BF)
    left = jnp.concatenate(
        [
            jnp.concatenate(
                [after_x[s * MX : (s + 1) * MX, hi * 128 : (hi + 1) * 128] for s in range(2 * LY)], 1
            )
            for hi in range(HI)
        ],
        0,
    )
    ready(waits, 1)
    after_y = dot(left, y_ref[...]) * scale
    grouped = jnp.concatenate(
        [
            jnp.concatenate(
                [
                    after_y[hi * MX + 8 * low : hi * MX + 8 * low + 8, t * 128 : (t + 1) * 128]
                    for low in range(4)
                ],
                1,
            )
            for t in range(2)
            for hi in range(HI)
        ],
        0,
    ).astype(BF)
    ready(waits, 3)
    spread = dot(grouped, spread_ref[...])
    found = {}
    for t in range(2):
        for hi in range(HI):
            for c in range(4):
                at = 4 * t + c
                row = (t * HI + hi) * 8
                found[hi * 4 + at // 2, at % 2] = spread[row : row + 8, c * 128 : (c + 1) * 128]
    return found


def modes_out(found, x_ref, y_back_ref, gather_ref, stage, out_ref, sems, waits):
    rows = []
    for t in range(2):
        for hi in range(HI):
            tiles = []
            for c in range(4):
                at = 4 * t + c
                tiles.append(found[hi * 4 + at // 2, at % 2])
            rows.append(jnp.concatenate(tiles, 1))
    ready(waits, 4)
    gathered = dot(jnp.concatenate(rows, 0).astype(BF), gather_ref[...])
    grouped = jnp.concatenate(
        [
            jnp.concatenate(
                [
                    gathered[(t * HI + hi) * 8 : (t * HI + hi) * 8 + 8, low * 128 : (low + 1) * 128]
                    for t in range(2)
                ],
                1,
            )
            for hi in range(HI)
            for low in range(4)
        ],
        0,
    ).astype(BF)
    ready(waits, 2)
    after_y = dot(grouped, y_back_ref[...]).astype(BF)
    left = jnp.concatenate(
        [
            jnp.concatenate(
                [
                    after_y[hi * MX : (hi + 1) * MX, s * 128 : (s + 1) * 128]
                    for hi in range(HI)
                ],
                1,
            )
            for s in range(2 * LY)
        ],
        0,
    )
    turned = left.T
    sent = []
    for j in range(0, GX, 2):
        after_x = dot(turned, x_ref[:, j * XY : (j + 2) * XY]).astype(BF)
        for e in range(2):
            for hi in range(HI):
                block = after_x[hi * 128 : (hi + 1) * 128, e * XY : (e + 1) * XY]
                stage[j + e, :, hi] = block.reshape(GY, 8, XY)
        part = pl.ds(j, 2)
        sent.append(pltpu.make_async_copy(stage.at[part], out_ref.at[part], sems.at[j // 2]))
        sent[-1].start()
    for copy in sent:
        copy.wait()


def mode_loads(tables_hbm, w_hbm, tables, w_ref, sems):
    groups = table_pairs(tables_hbm, tables)
    order = [groups[0], groups[1], groups[3], [(w_hbm, w_ref)], groups[4], groups[2]]
    moved = load([pair for group in order for pair in group], sems)
    split = []
    for group in order:
        split.append(moved[: len(group)])
        moved = moved[len(group) :]
    return [split[0], split[1], split[5], split[2], split[4]], split[3]


def mix_kernel(msg_ref, w_hbm, tables_hbm, out_ref, spec_ref, *scratch):
    x_ref, y_ref, y_back_ref, spread_ref, gather_ref, w_ref, stage, keep, mixed, unused, in_sems, sems = scratch
    waits, weights = mode_loads(tables_hbm, w_hbm, scratch[:5], w_ref, in_sems)
    spec = modes_in(msg_ref, x_ref, y_ref, spread_ref, 1.0, waits)
    for i in range(CH):
        for r in range(2):
            keep[i, r] = spec[i, r]
    kept = pltpu.make_async_copy(keep, spec_ref.at[0], sems.at[4])
    kept.start()
    weights[0].wait()

    def step(o, carry):
        real = jnp.zeros((8, 128), F32)
        imag = jnp.zeros((8, 128), F32)
        for i in range(CH):
            w_real = w_ref[0, i, o].astype(F32)
            w_imag = w_ref[1, i, o].astype(F32)
            real += w_real * keep[i, 0] - w_imag * keep[i, 1]
            imag += w_real * keep[i, 1] + w_imag * keep[i, 0]
        mixed[o, 0] = 4.0 * real
        mixed[o, 1] = 4.0 * imag
        return carry

    lax.fori_loop(0, CH, step, 0)
    modes_out(mixed, x_ref, y_back_ref, gather_ref, stage, out_ref, sems, waits)
    kept.wait()


def mix_back_kernel(msg_ref, w_hbm, tables_hbm, sums_hbm, out_ref, back_ref, *scratch):
    x_ref, y_ref, y_back_ref, spread_ref, gather_ref, w_ref, stage, keep, mixed, sums_ref, in_sems, sems = scratch
    waits, weights = mode_loads(tables_hbm, w_hbm, scratch[:5], w_ref, in_sems)
    fetched = pltpu.make_async_copy(sums_hbm.at[0], sums_ref, sems.at[5])
    fetched.start()
    back = modes_in(msg_ref, x_ref, y_ref, spread_ref, 4.0, waits)
    fetched.wait()
    for j in range(GX):
        stage[j, :, HI] = jnp.broadcast_to(sums_ref[...][None], (GY, 8, XY))
    for i in range(CH):
        for r in range(2):
            keep[i, r] = back[i, r]
    kept = pltpu.make_async_copy(keep, back_ref.at[0], sems.at[4])
    kept.start()
    weights[0].wait()

    def step(i, carry):
        real = jnp.zeros((8, 128), F32)
        imag = jnp.zeros((8, 128), F32)
        for o in range(CH):
            w_real = w_ref[0, i, o].astype(F32)
            w_imag = w_ref[1, i, o].astype(F32)
            real += w_real * keep[o, 0] + w_imag * keep[o, 1]
            imag += w_real * keep[o, 1] - w_imag * keep[o, 0]
        mixed[i, 0] = real
        mixed[i, 1] = imag
        return carry

    lax.fori_loop(0, CH, step, 0)
    modes_out(mixed, x_ref, y_back_ref, gather_ref, stage, out_ref, sems, waits)
    kept.wait()


def outer_kernel(spec_hbm, back_hbm, grad_ref, spec_ref, back_ref, sems):
    for copy in load([(spec_hbm.at[0], spec_ref), (back_hbm.at[0], back_ref)], sems):
        copy.wait()

    def step(i, carry):
        in_real = spec_ref[i, 0]
        in_imag = spec_ref[i, 1]
        for o in range(CH):
            real = back_ref[o, 0]
            imag = back_ref[o, 1]
            grad_ref[0, i, o] = (in_real * real + in_imag * imag).astype(BF)
            grad_ref[1, i, o] = (in_real * imag - in_imag * real).astype(BF)
        return carry

    lax.fori_loop(0, CH, step, 0)


def bypass_kernel(after_hbm, cells_ref, mix_ref, bias_ref, out_ref):
    for e in range(cells_ref.shape[1]):
        cells = cells_ref[:, e].reshape(CH * LY, ZT)
        total = dot(mix_ref[...], cells) + bias_ref[...]
        out_ref[:, e] = total.reshape(CH, LY, ZT).astype(BF)


def tail_kernel(
    msg_ref, bypass_hbm, cot_hbm, tables_hbm, out_ref, grad_out_ref, coef_ref,
    bypass_ref, cot_ref, inv_ref, back_ref, perm_ref, pack_ref,
    flat, coef, back_coef, stage, out_stage, grad_ref,
    in_sems, bypass_sems, cot_sems, sems, grad_sems, coef_sems,
):
    cells = 16
    rows = CH * cells
    root = math.sqrt(2.0 / math.pi)
    got = load(tail_pairs(tables_hbm, perm_ref, inv_ref, back_ref, pack_ref), in_sems)

    def part(g):
        return pl.ds(pl.multiple_of(g * cells, cells), cells)

    def bypass_copy(g):
        return pltpu.make_async_copy(bypass_hbm.at[:, part(g)], bypass_ref.at[:, part(g)], bypass_sems.at[g])

    def cot_copy(g):
        return pltpu.make_async_copy(cot_hbm.at[:, part(g)], cot_ref.at[:, part(g)], cot_sems.at[g])

    def out_copy(g):
        return pltpu.make_async_copy(out_stage.at[g], out_ref.at[:, part(g)], sems.at[g])

    def grad_copy(g):
        return pltpu.make_async_copy(grad_ref.at[:, part(g)], grad_out_ref.at[:, part(g)], grad_sems.at[g])

    for g in range(XY // cells):
        bypass_copy(g).start()
        cot_copy(g).start()
    got[0].wait()
    unpack(msg_ref, perm_ref, 2 * CH, flat, coef)
    for copy in got[1:]:
        copy.wait()

    def step(g, carry):
        bypass_copy(g).wait()
        cot_copy(g).wait()
        left = coef[:, part(g)].reshape(rows, PAIRS)
        back = jnp.zeros((rows, PAIRS), F32)
        for z in range(0, ZT, LANES):
            at = slice(z, z + LANES)
            bypass = bypass_ref[:, part(g), at].reshape(rows, LANES).astype(F32)
            pre = dot(left, inv_ref[:, at]) + bypass
            cot = cot_ref[:, part(g), at].reshape(rows, LANES)
            square = pre * pre
            bend = jnp.tanh(pre * (root + (root * 0.044715) * square))
            half = 0.5 + 0.5 * bend
            out_stage[g, :, :, at] = (pre * half).astype(BF).reshape(CH, cells, LANES)
            half = half.astype(BF)
            near = pre.astype(BF)
            rise = near * (BF(2.0 * root) + BF(6.0 * root * 0.044715) * (near * near))
            grad = cot * (half * (BF(1.0) + rise * (BF(1.0) - half)))
            grad_ref[:, part(g), at] = grad.reshape(CH, cells, LANES)
            back += dot(grad, back_ref[at])
        back_coef[:, part(g)] = back.astype(BF).reshape(CH, cells, PAIRS)
        out_copy(g).start()
        grad_copy(g).start()
        return carry

    def turn(n, carry):
        for e in range(4):
            ch = n * 4 + e
            flat[pl.ds(ch, 1)] = back_coef[ch].T[None]
        return carry

    def drain(g, carry):
        out_copy(g).wait()
        grad_copy(g).wait()
        return carry

    lax.fori_loop(0, XY // cells, step, 0, unroll=U[3])
    lax.fori_loop(0, CH // 4, turn, 0, unroll=U[2])
    pack(flat, pack_ref, stage, coef_ref, coef_sems)
    lax.fori_loop(0, XY // cells, drain, 0)


def sums_kernel(
    field_hbm, grad_hbm, fold_ref, sums_ref, field_ref, grad_ref, weight_sum, folds_ref, sems
):
    for copy in load([(field_hbm, field_ref), (grad_hbm, grad_ref)], sems):
        copy.wait()
    weight_sum[...] = jnp.zeros_like(weight_sum)

    def step(u, carry):
        field = field_ref[:, pl.ds(u, 1)].reshape(CH * LY, ZT)
        grad = grad_ref[:, pl.ds(u, 1)].reshape(CH * LY, ZT)
        ones = jnp.concatenate([field, jnp.ones((16, ZT), BF)], 0)
        weight_sum[...] += dot(ones, grad, ((1,), (1,)))
        return carry

    lax.fori_loop(0, LX, step, 0)
    summed = weight_sum[...]
    rows = lax.broadcasted_iota(jnp.int32, summed.shape, 0)
    lanes = lax.broadcasted_iota(jnp.int32, summed.shape, 1)
    keep = (rows >= CH * LY) | (rows % LY == lanes % LY)
    by_row = jnp.where(keep, summed, 0.0).reshape(CH + 2, LY, CH * LY)
    by_row = jnp.concatenate(
        [jnp.sum(by_row[:CH], 1), by_row[CH, :1], jnp.zeros((3, CH * LY), F32)], 0
    )
    at = lax.broadcasted_iota(jnp.int32, (CH * LY, 128), 0) // LY
    to = lax.broadcasted_iota(jnp.int32, (CH * LY, 128), 1)
    gather = jnp.where(at == to, 1.0, 0.0)
    full = lax.dot_general(
        by_row, gather, (((1,), (0,)), ((), ())),
        precision=lax.Precision.HIGHEST, preferred_element_type=F32,
    )
    high = full.astype(BF)
    low = (full - high.astype(F32)).astype(BF)
    both = jnp.concatenate([high.astype(F32), low.astype(F32)], 0).astype(BF)
    folded = jnp.zeros((8, 128), F32)
    for s in range(6):
        folded += pltpu.roll(dot(fold_ref[s], both), CH * s, 1)
    folds_ref[...] = folded.astype(BF)
    sent = pltpu.make_async_copy(folds_ref, sums_ref.at[0], sems.at[0])
    sent.start()
    sent.wait()


def last_kernel(
    msg_ref, bypass_hbm, tables_hbm, out_ref, weight_ref, bias_ref,
    bypass_ref, table_ref, perm_ref, fold_ref, flat, coef, out_stage, in_sems, bypass_sems, sems,
):
    cells = 16
    rows = CH * cells
    got = load(last_pairs(tables_hbm, perm_ref, table_ref, fold_ref), in_sems)

    def part(g):
        return pl.ds(pl.multiple_of(g * cells, cells), cells)

    def bypass_copy(g):
        return pltpu.make_async_copy(bypass_hbm.at[:, part(g)], bypass_ref.at[:, part(g)], bypass_sems.at[g])

    def out_copy(g):
        return pltpu.make_async_copy(out_stage.at[g], out_ref.at[:, part(g)], sems.at[g])

    for g in range(XY // cells):
        bypass_copy(g).start()
    got[0].wait()
    unpack(msg_ref, perm_ref, 48, flat, coef)
    for copy in got[1:]:
        copy.wait()

    def step(g, carry):
        bypass_copy(g).wait()
        left = coef[:, part(g)].reshape(rows, PAIRS)
        for z in range(0, ZT, LANES):
            at = slice(z, z + LANES)
            bypass = bypass_ref[:, part(g), at].reshape(rows, LANES).astype(F32)
            total = dot(left, table_ref[:, at]) + bypass
            out_stage[g, :, :, at] = total.astype(BF).reshape(CH, cells, LANES)
        out_copy(g).start()
        return carry

    lax.fori_loop(0, XY // cells, step, 0, unroll=U[3])

    def add(n, total):
        for e in range(8):
            at = pl.multiple_of((n * 8 + e) * 48 + 40, 8)
            total += msg_ref[pl.ds(at, 8)].astype(F32)
        return total

    summed = lax.fori_loop(0, MODES // 8, add, jnp.zeros((8, 128), F32))
    at = lax.broadcasted_iota(jnp.int32, (8, 128), 1)
    full = jnp.zeros((48, 128), F32)
    for s in range(6):
        own = jnp.where(at < CH, pltpu.roll(summed, (128 - CH * s) % 128, 1), 0.0)
        full += lax.dot_general(
            fold_ref[8 * s : 8 * s + 8, :48].astype(F32), own, (((0,), (0,)), ((), ())),
            precision=lax.Precision.HIGHEST, preferred_element_type=F32,
        )
    full = (full[:24] + full[24:]) * (1.0 / math.sqrt(NX * NY * ZT))
    weight_ref[...] = full[:CH, :CH]
    bias_ref[...] = full[CH : CH + 1, :CH]

    def drain(g, carry):
        out_copy(g).wait()
        return carry

    lax.fori_loop(0, XY // cells, drain, 0)


def exchange(messages):
    return lax.all_to_all(messages, AXES, split_axis=0, concat_axis=0, tiled=True)


DMA = pltpu.SemaphoreType.DMA
GRID = (CH, LX, LY, ZT)
MODE = (CH, 2, 8, 128)
TILES = (GX, GY, HI, 8, XY)
WIDE = (GX, GY, HI + 1, 8, XY)
MESSAGES = (MODES * 2 * CH, XY)
WEIGHT = (2, CH, CH, 8, 128)
MIX = (CH * LY, CH * LY)
FLOPS = 2 * CH * XY * ZT * PAIRS
FLAT = pltpu.VMEM((CH, PAIRS, XY), BF)
COEF = pltpu.VMEM((CH, XY, PAIRS), BF)
FLAT_GRID = (CH, XY, ZT)
CELLS = pltpu.VMEM(FLAT_GRID, BF)
OUT_STAGE = pltpu.VMEM((XY // 16, CH, 16, ZT), BF)
SLOTS = 13


def shaped(shape, kind=BF):
    return jax.ShapeDtypeStruct(shape, kind)


def mode_scratch(shape):
    kept = [pltpu.VMEM(WEIGHT, BF), pltpu.VMEM(shape, BF), pltpu.VMEM(MODE, F32), pltpu.VMEM(MODE, F32)]
    return table_scratch() + kept + [pltpu.VMEM((8, 128), BF), DMA((18,)), DMA((6,))]


def mix_stage(messages, weight, tables):
    return call(
        mix_kernel,
        (shaped(TILES), shaped((SLOTS, *MODE), F32)),
        limit=LIMITS[0],
        in_specs=[VMEM, HBM, HBM],
        out_specs=[HBM, HBM],
        scratch_shapes=mode_scratch(TILES),
    )(messages.reshape(TILES), weight, tables)


def bypass_stage(after, cells, mix, bias):
    block = pl.BlockSpec((CH, 2, LY, ZT), lambda g: (0, g, 0, 0))
    return call(
        bypass_kernel,
        shaped(GRID),
        limit=60,
        cost=(FLOPS, 2 * 5 * MIB),
        grid=(LX // 2,),
        in_specs=[HBM, block, pl.BlockSpec(MIX, lambda g: (0, 0)), pl.BlockSpec((CH * LY, 1), lambda g: (0, 0))],
        out_specs=block,
    )(after, cells, mix, bias).reshape(CH, XY, ZT)


def tail_stage(messages, bypass, cotangent, tables):
    perm = pltpu.VMEM((320, 384), BF)
    return call(
        tail_kernel,
        (shaped(FLAT_GRID), shaped(FLAT_GRID), shaped(MESSAGES)),
        limit=LIMITS[1],
        cost=(2 * FLOPS, 8 * 5 * MIB),
        in_specs=[VMEM] + [HBM] * 3,
        out_specs=[HBM, HBM, HBM],
        scratch_shapes=[
            CELLS, CELLS, pltpu.VMEM((PAIRS, ZT), BF), pltpu.VMEM((ZT, PAIRS), BF), perm, perm,
            FLAT, COEF, COEF, pltpu.VMEM(MESSAGES, BF), OUT_STAGE, CELLS,
            DMA((7,)), DMA((8,)), DMA((8,)), DMA((8,)), DMA((8,)), DMA((8,)),
        ],
    )(messages.reshape(MESSAGES), bypass, cotangent, tables)


def sums_stage(field, grad_pre, folds):
    return call(
        sums_kernel,
        shaped((1280, 8, 128)),
        limit=60,
        cost=(FLOPS, 2 * 5 * MIB),
        in_specs=[HBM, HBM, VMEM],
        out_specs=HBM,
        scratch_shapes=[pltpu.VMEM(GRID, BF)] * 2
        + [pltpu.VMEM((CH * LY + 16, CH * LY), F32), pltpu.VMEM((8, 128), BF), DMA((2,))],
    )(field, grad_pre, folds)


def mix_back_stage(messages, weight, tables, sums):
    return call(
        mix_back_kernel,
        (shaped(WIDE), shaped((SLOTS, *MODE), F32)),
        limit=LIMITS[2],
        in_specs=[VMEM, HBM, HBM, HBM],
        out_specs=[HBM, HBM],
        scratch_shapes=mode_scratch(WIDE),
    )(messages.reshape(TILES), weight, tables, sums)


def outer_stage(spec, modes_back):
    return call(
        outer_kernel,
        shaped(WEIGHT),
        limit=60,
        cost=(8 * CH * CH * 1024, 2 * MIB),
        in_specs=[HBM, HBM],
        scratch_shapes=[pltpu.VMEM(MODE, F32), pltpu.VMEM(MODE, F32), DMA((2,))],
    )(spec, modes_back)


def last_stage(messages, bypass, tables):
    return call(
        last_kernel,
        (shaped(FLAT_GRID), shaped((CH, CH), F32), shaped((1, CH), F32)),
        limit=LIMITS[3],
        cost=(FLOPS, 2 * 5 * MIB),
        in_specs=[VMEM, HBM, HBM],
        out_specs=[HBM, VMEM, VMEM],
        scratch_shapes=[
            CELLS, pltpu.VMEM((PAIRS, ZT), BF), pltpu.VMEM((320, 384), BF), pltpu.VMEM((48, 128), BF),
            FLAT, COEF, OUT_STAGE, DMA((3,)), DMA((8,)), DMA((8,)),
        ],
    )(messages.reshape(MODES * 48, XY), bypass, tables)


def local(field, spectral_weight, bypass_weight, bypass_bias, cotangent):
    eye = jnp.eye(LY, dtype=BF)
    mix_in = jnp.kron(bypass_weight, eye)
    mix_out = jnp.kron(bypass_weight.T, eye)
    bias = jnp.repeat(bypass_bias, LY)[:, None]
    tables = const(mode_tables())
    weight = spectral_weight.reshape(WEIGHT)

    plane = plane_stage(field.reshape(FLAT_GRID), const(plane_tables()[0]), const(pack_table(40)))
    arrived = exchange(plane.reshape(MODES, 2 * CH, XY))
    bypass = bypass_stage(plane, field, mix_out, bias)
    sent, spec = mix_stage(arrived, weight, tables)
    arrived = exchange(sent.reshape(MODES, 2 * CH, XY))
    out_field, grad_pre, back_coef = tail_stage(
        arrived, bypass, cotangent.reshape(FLAT_GRID), const(tail_tables())
    )
    grad_pre = grad_pre.reshape(GRID)
    arrived = exchange(back_coef.reshape(MODES, 2 * CH, XY))
    sums = sums_stage(field, grad_pre, const(fold_table()))
    sent, modes_back = mix_back_stage(arrived, weight, tables, sums)
    arrived = exchange(sent.reshape(MODES, 48, XY))
    bypass = bypass_stage(back_coef, grad_pre, mix_in, jnp.zeros_like(bias))
    spectral_grad = outer_stage(spec, modes_back).reshape(spectral_weight.shape)
    field_grad, weight_grad, bias_grad = last_stage(arrived, bypass, const(last_tables()))
    return (
        out_field.reshape(GRID), field_grad.reshape(GRID), spectral_grad, weight_grad, bias_grad.reshape(CH),
    )


def solution(mesh):
    in_specs = (
        P(None, "gx", "gy", None),
        P(None, AXES, None, None, None),
        P(),
        P(),
        P(None, "gx", "gy", None),
    )
    out_specs = (
        P(None, "gx", "gy", None),
        P(None, "gx", "gy", None),
        P(None, AXES, None, None, None),
        P(),
        P(),
    )
    return jax.shard_map(local, mesh=mesh, in_specs=in_specs, out_specs=out_specs, check_vma=False)
```
